512 devices in a mesh: dp: 64 (over y, z), tensor: 8 (over x, core).
Axes of the slice: x: 4, y: 4, z: 16, core: 2. Of those that a mesh axis runs over, the one named last changes fastest.
Arguments:
- inputs: bfloat16 [65536, 5120], P(('dp', 'tensor')), may hold values from -6 to 6
- out_grad: bfloat16 [65536, 5120], P(('dp', 'tensor')), may hold values from -6 to 6
- hidden: bfloat16 [65536, 256], P('dp', 'tensor'), may hold values from -0.1875 to 0.1875
- up_grad: bfloat16 [65536, 256], P('dp', 'tensor'), may hold values from -0.1875 to 0.1875
- gate_grad: bfloat16 [65536, 256], P('dp', 'tensor'), may hold values from -0.1875 to 0.1875
- error_memory: bfloat16 [64, 3, 256, 5120], P('dp', None, 'tensor'), may hold values from -3 to 3
- q_start: bfloat16 [3, 32, 5120], replicated, may hold values from -0.078125 to 0.078125
Outputs:
- error_next: bfloat16 [64, 3, 256, 5120], P('dp', None, 'tensor')
- p_factor: float32 [3, 256, 32], P(None, 'tensor')
- q_factor: bfloat16 [3, 32, 5120], replicated
The draws below stay inside these ranges and needn't reach their ends.
All inputs are finite; a program needn't handle non-finite values.
Results may differ from the reference program's by a relative error of at most 0.0016.
Values may be sent and summed in bfloat16 or wider, within the bound.
No kernel may reach another device: no remote copies, remote signals or barrier semaphores. Data moves between devices by JAX's collectives and lax.ppermute only.
A program may use at most 128 MiB of HBM per device.

```python
import jax
import jax.numpy as jnp
from jax import lax

D = 5120
RANK = 32
TOK = 1024
TOKENS = 65536
FF_WIN = 256
REPLICAS = 64


def levels(own_key, dims, shards, smallest, high):
    loudness = 1.0
    for axis_at, shards_of in shards:
        heights = jax.random.uniform(jax.random.fold_in(jax.random.fold_in(own_key, 6), axis_at), (shards_of,), jnp.float32, smallest / len(shards), high / len(shards))
        loudness = loudness * jnp.repeat(jnp.exp(heights), dims[axis_at] // shards_of).reshape((-1,) + (1,) * (len(dims) - 1 - axis_at))
    return loudness


def bell_draw(rng, shape, scale, reach, shards=(), dtype=jnp.bfloat16):
    drawn = jax.random.normal(rng, shape, jnp.float32) * scale
    if len(shards) > 0:
        drawn = levels(rng, shape, shards, -0.22, 0.18) * drawn
    return jnp.clip(drawn, min=-reach, max=reach).astype(dtype)


def setup_inputs(seed: int = 0) -> dict:
    key_of = jax.random.split(jax.random.key(seed), 8)
    inputs = bell_draw(key_of[0], (TOKENS, D), 1.0, 6.0, ((0, 512),))
    out_grad = bell_draw(key_of[1], (TOKENS, D), 1.0, 6.0, ((0, 512),))
    hidden = bell_draw(key_of[2], (TOKENS, FF_WIN), TOK ** -0.5, 0.1875, ((0, 64), (1, 8)))
    up_grad = bell_draw(key_of[3], (TOKENS, FF_WIN), TOK ** -0.5, 0.1875, ((0, 64), (1, 8)))
    gate_grad = bell_draw(key_of[4], (TOKENS, FF_WIN), TOK ** -0.5, 0.1875, ((0, 64), (1, 8)))
    error_memory = bell_draw(key_of[5], (REPLICAS, 3, FF_WIN, D), 0.5, 3.0, ((0, 64), (2, 8)))
    q_start = bell_draw(key_of[6], (3, RANK, D), D ** -0.5, 0.078125)
    return {"inputs": inputs, "out_grad": out_grad, "hidden": hidden, "up_grad": up_grad, "gate_grad": gate_grad, "error_memory": error_memory, "q_start": q_start}


PRECISE = lax.Precision.HIGHEST

def orthonormal(p_rows, gram_matrix):
    factor = jnp.linalg.cholesky(gram_matrix)
    solved = jax.scipy.linalg.solve_triangular(factor, p_rows.T, lower=True)
    return solved.T

def replica_matrices(operands):
    inputs, out_grad, hidden, up_grad, gate_grad, error_memory = operands
    branch_grads = jnp.concatenate([up_grad, gate_grad], axis=1)
    branch = jnp.dot(branch_grads.T.astype(jnp.float32), inputs.astype(jnp.float32), preferred_element_type=jnp.float32)
    down = jnp.dot(hidden.T.astype(jnp.float32), out_grad.astype(jnp.float32), preferred_element_type=jnp.float32)
    stacked = jnp.concatenate([branch, down], axis=0).reshape(3, FF_WIN, D)
    return stacked + error_memory.astype(jnp.float32)

def reference(inputs, out_grad, hidden, up_grad, gate_grad, error_memory, q_start):
    operands = (inputs.reshape(REPLICAS, TOK, D), out_grad.reshape(REPLICAS, TOK, D), hidden.reshape(REPLICAS, TOK, FF_WIN), up_grad.reshape(REPLICAS, TOK, FF_WIN), gate_grad.reshape(REPLICAS, TOK, FF_WIN), error_memory)
    matrices = lax.map(replica_matrices, operands)
    q_float = q_start.astype(jnp.float32)
    p_sum = jnp.einsum('kmfd,mrd->mfr', matrices, q_float, precision=PRECISE)
    gram_matrix = jnp.einsum('mfr,mfs->mrs', p_sum, p_sum, precision=PRECISE)
    p_factor = jax.vmap(orthonormal)(p_sum, gram_matrix)
    q_sum = jnp.einsum('mfr,kmfd->mrd', p_factor, matrices, precision=PRECISE)
    q_factor = (q_sum / REPLICAS).astype(jnp.bfloat16)
    q_used = lax.optimization_barrier(q_factor).astype(jnp.float32)
    rebuilt = jnp.einsum('mfr,mrd->mfd', p_factor, q_used, precision=PRECISE)
    error_next = (matrices - rebuilt[None]).astype(jnp.bfloat16)
    return (error_next, p_factor, q_factor)
```

```python
import jax
import jax.numpy as jnp
from jax import lax
from jax.sharding import Mesh, PartitionSpec as P

PRECISE = lax.Precision.HIGHEST
NY, NZ, NX, NC = 4, 16, 4, 2


def spread(value, axis, count):
    copies = jnp.broadcast_to(value[None], (count,) + value.shape)
    return lax.all_to_all(copies, axis, 0, 0)


def swap_core(value):
    return lax.ppermute(value, "c", [(0, 1), (1, 0)])


def sum_tensor(value):
    value = value + swap_core(value)
    value = value + lax.ppermute(value, "x", [(i, i ^ 1) for i in range(NX)])
    return value + lax.ppermute(value, "x", [(i, i ^ 2) for i in range(NX)])


def inverse_factor(gram_matrix):
    factor = jnp.linalg.cholesky(gram_matrix)
    unit = jnp.eye(gram_matrix.shape[0], dtype=jnp.float32)
    return jax.scipy.linalg.solve_triangular(factor, unit, lower=True)


def per_device(inputs, out_grad, hidden, up_grad, gate_grad, error_memory, q_start):
    row_count = hidden.shape[1]
    width = inputs.shape[1]
    rank = q_start.shape[1]
    core = lax.axis_index("c")
    branch_grads = jnp.concatenate([up_grad, gate_grad], axis=1)
    branch_term = jnp.dot(
        branch_grads.T,
        lax.all_gather(inputs, ("x", "c"), axis=0, tiled=True),
        preferred_element_type=jnp.float32,
    )
    down_term = jnp.dot(
        hidden.T,
        lax.all_gather(out_grad, ("x", "c"), axis=0, tiled=True),
        preferred_element_type=jnp.float32,
    )
    matrices = jnp.concatenate([branch_term, down_term], axis=0).reshape(3, row_count, width)
    matrices = matrices + error_memory[0].astype(jnp.float32)
    q_float = q_start.astype(jnp.float32)
    p_part = jnp.einsum("mfd,mrd->mfr", matrices, q_float, precision=PRECISE)
    p_flat = p_part.reshape(24, 128)
    p_flat = spread(p_flat, "z", NZ).sum(0)
    p_flat = spread(p_flat, "y", NY).sum(0)
    p_local = p_flat.reshape(3, row_count, rank)

    gram_part = jnp.einsum("mfr,mfs->mrs", p_local, p_local, precision=PRECISE)
    inverse = jax.vmap(inverse_factor)(sum_tensor(gram_part))

    half = width // NC
    blocks = half // NX // 128
    w_part = jnp.einsum("mfr,mfd->mrd", p_local, matrices, precision=PRECISE)
    mine = lax.dynamic_slice_in_dim(w_part, core * half, half, axis=2)
    theirs = lax.dynamic_slice_in_dim(w_part, (1 - core) * half, half, axis=2)
    w_core = mine + swap_core(theirs)
    w_core = w_core.reshape(3, rank, NX, blocks, 128).transpose(2, 0, 3, 1, 4)
    w_x = lax.all_to_all(w_core.reshape(NX, 3 * blocks * rank, 128), "x", 0, 0).sum(0)
    w_x = jnp.pad(w_x, ((0, rank), (0, 0))).reshape(NY, 4 * rank, 128)
    w_y = lax.all_to_all(w_x, "y", 0, 0).sum(0).reshape(4, rank, 128)
    unit_of = jnp.minimum((lax.axis_index("y") * 4 + jnp.arange(4)) // blocks, 2)
    q_y = jnp.einsum("urs,usd->urd", inverse[unit_of], w_y, precision=PRECISE)
    q_z = lax.all_to_all(q_y.reshape(NZ, 8, 128), "z", 0, 0).sum(0)
    q_part = (q_z / (NY * NZ)).astype(jnp.bfloat16)

    q_dp = spread(q_part, ("y", "z"), NY * NZ).reshape(NY * NZ * 8, 128)
    q_x = spread(q_dp[: 3 * blocks * rank], "x", NX)
    q_other = swap_core(q_x)
    first = core == 0
    q_all = jnp.stack([jnp.where(first, q_x, q_other), jnp.where(first, q_other, q_x)])
    q_all = q_all.reshape(NC, NX, 3, blocks, rank, 128).transpose(2, 4, 0, 1, 3, 5)
    q_factor = q_all.reshape(3, rank, width)

    p_factor = jnp.einsum("mfr,msr->mfs", p_local, inverse, precision=PRECISE)
    q_used = lax.optimization_barrier(q_factor).astype(jnp.float32)
    rebuilt = jnp.einsum("mfr,mrd->mfd", p_factor, q_used, precision=PRECISE)
    error_next = (matrices - rebuilt).astype(jnp.bfloat16)[None]
    return (error_next, p_factor, q_factor)


def solution(mesh):
    fine = Mesh(mesh.devices.reshape(NY, NZ, NX, NC), ("y", "z", "x", "c"))
    dp, tensor = ("y", "z"), ("x", "c")
    in_specs = (
        P(dp + tensor, None),
        P(dp + tensor, None),
        P(dp, tensor),
        P(dp, tensor),
        P(dp, tensor),
        P(dp, None, tensor, None),
        P(),
    )
    out_specs = (P(dp, None, tensor, None), P(None, tensor, None), P())
    return jax.shard_map(
        per_device, mesh=fine, in_specs=in_specs, out_specs=out_specs, check_vma=False
    )
```

```python
import jax
import jax.numpy as jnp
from jax import lax
from jax.experimental import pallas as pl
from jax.experimental.pallas import tpu as pltpu
from jax.sharding import Mesh, PartitionSpec as P

NY, NZ, NX, NC = 4, 16, 4, 2
D = 5120
RANK = 32
ROWS = 32
CHUNKS = 4
WIDE = D // CHUNKS
HALF = D // NC
PIECE = HALF // NX
BLOCKS = PIECE // 128
UNITS = 3 * BLOCKS
F32, BF16 = jnp.float32, jnp.bfloat16
VMEM_BYTES = 48 * 1024 * 1024
PRECISE = lax.Precision.HIGHEST


def params():
    return pltpu.CompilerParams(vmem_limit_bytes=VMEM_BYTES)


def split3(value):
    high = value.astype(BF16)
    rest = value - high.astype(F32)
    middle = rest.astype(BF16)
    low = (rest - middle.astype(F32)).astype(BF16)
    return high, middle, low


def pack_rows(p_rows):
    packed = p_rows[0:8]
    for group in range(1, 4):
        packed = packed + pltpu.roll(p_rows[8 * group : 8 * group + 8], 32 * group, 1)
    return packed


def unpack_rows(packed):
    parts = [packed] + [pltpu.roll(packed, 128 - 32 * group, 1) for group in range(1, 4)]
    return jnp.concatenate(parts, axis=0)[:, :RANK]


def partial_kernel(u_self, u_far, own, sibling, pair, pair_sibling, error, mine, far):
    for at, first, last in ((0, 0, 2), (1, 2, 3)):
        tokens = jnp.concatenate([own[at], sibling[at], pair[at], pair_sibling[at]], axis=0)
        rows = slice(first * ROWS, last * ROWS)
        columns = jnp.concatenate([u_self[rows, :], u_far[rows, :]], axis=0)
        sums = jnp.dot(columns, tokens, preferred_element_type=F32)
        count = last - first
        for k in range(count):
            mine[first + k] = sums[k * ROWS : (k + 1) * ROWS] + error[0, first + k].astype(F32)
            far[first + k] = sums[(count + k) * ROWS : (count + k + 1) * ROWS]


def partials(u_self, u_far, own, sibling, pair, pair_sibling, error, chunk):
    steps = 2
    width = WIDE // steps
    u_spec = pl.BlockSpec((3 * ROWS, 512), lambda i: (0, 0))
    x_spec = pl.BlockSpec((2, 128, width), lambda i: (0, 0, i))
    e_spec = pl.BlockSpec((1, 3, ROWS, width), lambda i: (0, 0, 0, chunk * steps + i))
    o_spec = pl.BlockSpec((3, ROWS, width), lambda i: (0, 0, i))
    shape = jax.ShapeDtypeStruct((3, ROWS, WIDE), F32)
    return pl.pallas_call(
        partial_kernel,
        grid=(steps,),
        in_specs=[u_spec, u_spec, x_spec, x_spec, x_spec, x_spec, e_spec],
        out_specs=[o_spec, o_spec],
        out_shape=[shape, shape],
        compiler_params=params(),
        name="partial_gradients",
    )(u_self, u_far, own, sibling, pair, pair_sibling, error)


def left_kernel(*refs):
    mine, far, q_ref = refs[:CHUNKS], refs[CHUNKS : 2 * CHUNKS], refs[2 * CHUNKS]
    matrices, packed = refs[2 * CHUNKS + 1 :]
    total = jnp.zeros((3 * ROWS, 128), F32)
    for chunk in range(CHUNKS):
        columns = slice(chunk * WIDE, (chunk + 1) * WIDE)
        value = mine[chunk][0] + far[chunk][0]
        matrices[0, :, columns] = value
        stacked = jnp.concatenate(split3(value), axis=0)
        right = jnp.concatenate([q_ref[0, :, columns], jnp.zeros((128 - RANK, WIDE), BF16)], axis=0)
        total = total + lax.dot_general(
            stacked, right, (((1,), (1,)), ((), ())), preferred_element_type=F32
        )
    p_rows = total[:ROWS] + (total[ROWS : 2 * ROWS] + total[2 * ROWS :])
    packed[0] = pack_rows(p_rows)


def left_product(mine, far, q_start):
    chunk_spec = pl.BlockSpec((1, ROWS, WIDE), lambda m: (m, 0, 0))
    wide_spec = pl.BlockSpec((1, ROWS, D), lambda m: (m, 0, 0))
    return pl.pallas_call(
        left_kernel,
        grid=(3,),
        in_specs=[chunk_spec] * (2 * CHUNKS) + [wide_spec],
        out_specs=[wide_spec, pl.BlockSpec((1, 8, 128), lambda m: (m, 0, 0))],
        out_shape=[
            jax.ShapeDtypeStruct((3, ROWS, D), F32),
            jax.ShapeDtypeStruct((3, 8, 128), F32),
        ],
        compiler_params=params(),
        name="left_product",
    )(*mine, *far, q_start)


def right_kernel(core_ref, packed, matrices, mine, theirs, gram):
    core = core_ref[0]
    p_rows = unpack_rows(packed[0])
    gram[0] = lax.dot_general(
        p_rows, p_rows, (((0,), (0,)), ((), ())), preferred_element_type=F32, precision=PRECISE
    )
    high, middle, low = split3(p_rows)
    left = jnp.concatenate([high, high, middle, high, low, middle], axis=0)
    for out, half in ((mine, core), (theirs, 1 - core)):
        for at in range(NX):
            start = pl.multiple_of(half * HALF + at * PIECE, 128)
            high, middle, low = split3(matrices[0, :, pl.ds(start, PIECE)])
            right = jnp.concatenate([high, middle, high, low, high, middle], axis=0)
            product = lax.dot_general(
                left, right, (((0,), (0,)), ((), ())), preferred_element_type=F32
            )
            for block in range(BLOCKS):
                out[at, block] = product[:, block * 128 : (block + 1) * 128]


def right_product(core, packed, matrices):
    out_spec = pl.BlockSpec((NX, BLOCKS, RANK, 128), lambda m: (0, m, 0, 0))
    out_shape = jax.ShapeDtypeStruct((NX, UNITS, RANK, 128), F32)
    return pl.pallas_call(
        right_kernel,
        grid=(3,),
        in_specs=[
            pl.BlockSpec(memory_space=pltpu.SMEM),
            pl.BlockSpec((1, 8, 128), lambda m: (m, 0, 0)),
            pl.BlockSpec((1, ROWS, D), lambda m: (m, 0, 0)),
        ],
        out_specs=[out_spec, out_spec, pl.BlockSpec((1, RANK, RANK), lambda m: (m, 0, 0))],
        out_shape=[out_shape, out_shape, jax.ShapeDtypeStruct((3, RANK, RANK), F32)],
        compiler_params=params(),
        name="right_product",
    )(core, packed, matrices)


def factor_kernel(gram, packed, inverse, p_factor):
    lane = lax.broadcasted_iota(jnp.int32, (3, RANK, RANK), 2)
    row = lax.broadcasted_iota(jnp.int32, (3, RANK, RANK), 1)
    left = gram[...]
    right = jnp.where(lane == row, 1.0, 0.0).astype(F32)
    for step in range(RANK):
        pivot = left[:, step : step + 1, :]
        column = left[:, :, step : step + 1] / pivot[:, :, step : step + 1]
        scale = jnp.where(row[:, :, :1] > step, column, 0.0)
        right = right - scale * right[:, step : step + 1, :]
        left = left - scale * pivot
    diagonal = jnp.sum(jnp.where(lane == row, left, 0.0), axis=2, keepdims=True)
    result = right / jnp.sqrt(diagonal)
    inverse[...] = result
    for m in range(3):
        p_factor[m] = lax.dot_general(
            unpack_rows(packed[m]),
            result[m],
            (((1,), (1,)), ((), ())),
            preferred_element_type=F32,
            precision=PRECISE,
        )


def factors(gram, packed):
    shape = jax.ShapeDtypeStruct((3, RANK, RANK), F32)
    return pl.pallas_call(
        factor_kernel,
        out_shape=[shape, shape],
        compiler_params=params(),
        name="factors",
    )(gram, packed)


def error_kernel(core_ref, q_near, q_far, p_factor, matrices, q_factor, error_next):
    core = core_ref[0]
    left = jnp.concatenate(split3(p_factor[0]), axis=1)
    for part, half in ((q_near, core), (q_far, 1 - core)):
        for at in range(NX):
            start = pl.multiple_of(half * HALF + at * PIECE, 128)
            columns = pl.ds(start, PIECE)
            right = jnp.concatenate([part[at, block] for block in range(BLOCKS)], axis=1)
            q_factor[0, :, columns] = right
            rebuilt = jnp.dot(
                left, jnp.concatenate([right] * 3, axis=0), preferred_element_type=F32
            )
            error_next[0, 0, :, columns] = (matrices[0, :, columns] - rebuilt).astype(BF16)


def new_error(core, q_near, q_far, p_factor, matrices):
    q_spec = pl.BlockSpec((NX, BLOCKS, RANK, 128), lambda m: (0, m, 0, 0))
    wide_spec = pl.BlockSpec((1, ROWS, D), lambda m: (m, 0, 0))
    return pl.pallas_call(
        error_kernel,
        grid=(3,),
        in_specs=[
            pl.BlockSpec(memory_space=pltpu.SMEM),
            q_spec,
            q_spec,
            pl.BlockSpec((1, ROWS, RANK), lambda m: (m, 0, 0)),
            wide_spec,
        ],
        out_specs=[wide_spec, pl.BlockSpec((1, 1, ROWS, D), lambda m: (0, m, 0, 0))],
        out_shape=[
            jax.ShapeDtypeStruct((3, RANK, D), BF16),
            jax.ShapeDtypeStruct((1, 3, ROWS, D), BF16),
        ],
        compiler_params=params(),
        name="new_error",
    )(core, q_near, q_far, p_factor, matrices)


def spread(value, axis, count):
    copies = jnp.broadcast_to(value[None], (count,) + value.shape)
    return lax.all_to_all(copies, axis, 0, 0)


def swap_core(value):
    return lax.ppermute(value, "c", [(0, 1), (1, 0)])


def neighbour(at, way):
    return 3 - at if way else at ^ 1


def swap_chip(value, way):
    return lax.ppermute(value, "x", [(i, neighbour(i, way)) for i in range(NX)])


def sum_tensor(value):
    value = value + swap_core(value)
    value = value + lax.ppermute(value, "x", [(i, i ^ 1) for i in range(NX)])
    return value + lax.ppermute(value, "x", [(i, i ^ 2) for i in range(NX)])


def exchange(inputs, out_grad, hidden, up_grad, gate_grad, error_memory):
    chip, core = lax.axis_index("x"), lax.axis_index("c")
    columns = jnp.concatenate([up_grad.T, gate_grad.T, hidden.T], axis=0)

    def tokens_of(first, second):
        starts = [(at * 2 + side) * 128 for at in (first, second) for side in (core, 1 - core)]
        return jnp.concatenate(
            [lax.dynamic_slice_in_dim(columns, start, 128, axis=1) for start in starts], axis=1
        )

    own = [
        jnp.stack([inputs[:, k * WIDE : (k + 1) * WIDE], out_grad[:, k * WIDE : (k + 1) * WIDE]])
        for k in range(CHUNKS)
    ]
    order = (0, 2, 1, 3)
    pair = {k: swap_chip(own[k], k // 2) for k in order}
    u_self, u_far = [], []
    for way in range(2):
        partner = neighbour(chip, 1 - way)
        u_self.append(tokens_of(chip, neighbour(chip, way)))
        u_far.append(swap_chip(tokens_of(partner, neighbour(partner, way)), 1 - way))
    sibling = {k: swap_core(own[k]) for k in order}
    mine, far = {}, {}
    for k in order:
        way = k // 2
        pair_sibling = swap_core(pair[k])
        mine[k], sent = partials(
            u_self[way], u_far[way], own[k], sibling[k], pair[k], pair_sibling, error_memory, k
        )
        far[k] = swap_chip(sent, 1 - way)
    return [mine[k] for k in range(CHUNKS)], [far[k] for k in range(CHUNKS)]


def per_device(inputs, out_grad, hidden, up_grad, gate_grad, error_memory, q_start):
    core = lax.axis_index("c").reshape(1).astype(jnp.int32)
    mine, far = exchange(inputs, out_grad, hidden, up_grad, gate_grad, error_memory)
    matrices, packed = left_product(mine, far, q_start)

    packed = spread(packed, "z", NZ).sum(0)
    packed = spread(packed, "y", NY).sum(0)

    near, away, gram_part = right_product(core, packed, matrices)
    w_core = near + swap_core(away)
    inverse, p_factor = factors(sum_tensor(gram_part), packed)
    w_x = lax.all_to_all(w_core.reshape(NX, UNITS * RANK, 128), "x", 0, 0).sum(0)
    w_x = jnp.pad(w_x, ((0, RANK), (0, 0))).reshape(NY, 4 * RANK, 128)
    w_y = lax.all_to_all(w_x, "y", 0, 0).sum(0).reshape(4, RANK, 128)
    unit_of = jnp.minimum((lax.axis_index("y") * 4 + jnp.arange(4)) // BLOCKS, 2)
    q_y = jnp.einsum("urs,usd->urd", inverse[unit_of], w_y, precision=PRECISE)
    q_z = lax.all_to_all(q_y.reshape(NZ, 8, 128), "z", 0, 0).sum(0)
    q_part = (q_z / (NY * NZ)).astype(BF16)

    q_dp = spread(q_part, ("y", "z"), NY * NZ).reshape(NY * NZ * 8, 128)
    q_x = spread(q_dp[: UNITS * RANK], "x", NX).reshape(NX, UNITS, RANK, 128)
    q_factor, error_next = new_error(core, q_x, swap_core(q_x), p_factor, matrices)
    return (error_next, p_factor, q_factor)


def solution(mesh):
    fine = Mesh(mesh.devices.reshape(NY, NZ, NX, NC), ("y", "z", "x", "c"))
    dp, tensor = ("y", "z"), ("x", "c")
    in_specs = (
        P(dp + tensor, None),
        P(dp + tensor, None),
        P(dp, tensor),
        P(dp, tensor),
        P(dp, tensor),
        P(dp, None, tensor, None),
        P(),
    )
    out_specs = (P(dp, None, tensor, None), P(None, tensor, None), P())
    return jax.shard_map(
        per_device, mesh=fine, in_specs=in_specs, out_specs=out_specs, check_vma=False
    )
```

```python
import jax
import jax.numpy as jnp
from jax import lax
from jax.experimental import pallas as pl
from jax.experimental.pallas import tpu as pltpu
from jax.sharding import Mesh, PartitionSpec as P

NY, NZ, NX, NC = 4, 16, 4, 2
D = 5120
RANK = 32
ROWS = 32
HALF = D // NC
PIECE = HALF // NX
BLOCKS = PIECE // 128
UNITS = 3 * BLOCKS
F32, BF16 = jnp.float32, jnp.bfloat16
VMEM_BYTES = 48 * 1024 * 1024
PRECISE = lax.Precision.HIGHEST


def params():
    return pltpu.CompilerParams(vmem_limit_bytes=VMEM_BYTES)


def split3(value):
    high = value.astype(BF16)
    rest = value - high.astype(F32)
    middle = rest.astype(BF16)
    low = (rest - middle.astype(F32)).astype(BF16)
    return high, middle, low


def pack_rows(p_rows):
    packed = p_rows[0:8]
    for group in range(1, 4):
        packed = packed + pltpu.roll(p_rows[8 * group : 8 * group + 8], 32 * group, 1)
    return packed


def unpack_rows(packed):
    parts = [packed] + [pltpu.roll(packed, 128 - 32 * group, 1) for group in range(1, 4)]
    return jnp.concatenate(parts, axis=0)


def partial_kernel(u_self, u_far, own, sibling, pair, pair_sibling, error, q_ref, mine, far, p_mine, p_far, total):
    step = pl.program_id(0)

    @pl.when(step == 0)
    def _():
        total[...] = jnp.zeros_like(total)

    width = own.shape[2]
    for at, first, last in ((0, 0, 2), (1, 2, 3)):
        tokens = jnp.concatenate([own[at], sibling[at], pair[at], pair_sibling[at]], axis=0)
        rows = slice(first * ROWS, last * ROWS)
        columns = jnp.concatenate([u_self[rows, :], u_far[rows, :]], axis=0)
        sums = jnp.dot(columns, tokens, preferred_element_type=F32)
        count = last - first
        for k in range(count):
            m = first + k
            mine_m = sums[k * ROWS : (k + 1) * ROWS] + error[0, m].astype(F32)
            far_m = sums[(count + k) * ROWS : (count + k + 1) * ROWS]
            mine[m] = mine_m
            far[m] = far_m
            stacked = jnp.concatenate(split3(mine_m) + split3(far_m), axis=0)
            right = jnp.concatenate([q_ref[m], jnp.zeros((128 - RANK, width), BF16)], axis=0)
            total[m] += lax.dot_general(
                stacked, right, (((1,), (1,)), ((), ())), preferred_element_type=F32
            )

    @pl.when(step == pl.num_programs(0) - 1)
    def _():
        for m in range(3):
            for at, out in ((0, p_mine), (3, p_far)):
                parts = [total[m, (at + k) * ROWS : (at + k + 1) * ROWS] for k in range(3)]
                out[m] = pack_rows(parts[0] + (parts[1] + parts[2]))


def partials(u_self, u_far, own, sibling, pair, pair_sibling, error, q_start, way):
    steps = 4
    width = HALF // steps
    u_spec = pl.BlockSpec((3 * ROWS, 512), lambda i: (0, 0))
    x_spec = pl.BlockSpec((2, 128, width), lambda i: (0, 0, i))
    e_spec = pl.BlockSpec((1, 3, ROWS, width), lambda i: (0, 0, 0, way * steps + i))
    q_spec = pl.BlockSpec((3, RANK, width), lambda i: (0, 0, way * steps + i))
    o_spec = pl.BlockSpec((3, ROWS, width), lambda i: (0, 0, i))
    p_spec = pl.BlockSpec((3, 8, 128), lambda i: (0, 0, 0))
    shape = jax.ShapeDtypeStruct((3, ROWS, HALF), F32)
    p_shape = jax.ShapeDtypeStruct((3, 8, 128), F32)
    return pl.pallas_call(
        partial_kernel,
        grid=(steps,),
        in_specs=[u_spec, u_spec, x_spec, x_spec, x_spec, x_spec, e_spec, q_spec],
        out_specs=[o_spec, o_spec, p_spec, p_spec],
        out_shape=[shape, shape, p_shape, p_shape],
        scratch_shapes=[pltpu.VMEM((3, 6 * ROWS, 128), F32)],
        compiler_params=params(),
        name="partial_gradients",
    )(u_self, u_far, own, sibling, pair, pair_sibling, error, q_start)


def right_kernel(core_ref, packed, mine_0, far_0, mine_1, far_1, near, away):
    m = pl.program_id(0)
    first = core_ref[0] == 0
    wide = unpack_rows(packed[0])
    lane = lax.broadcasted_iota(jnp.int32, wide.shape, 1)
    wide = jnp.where(lane < RANK, wide, 0.0)
    p_rows = wide[:, :RANK]
    gram = lax.dot_general(
        p_rows,
        pltpu.roll(wide, RANK * m, 1),
        (((0,), (0,)), ((), ())),
        preferred_element_type=F32,
        precision=PRECISE,
    )
    for out in (near, away):
        for at in range(NX):
            out[at, UNITS] = jnp.where(m == 0, gram, out[at, UNITS] + gram)
    high, middle, low = split3(p_rows)
    left = jnp.concatenate([high, high, middle, high, low, middle], axis=0)
    for at in range(NX):
        columns = slice(at * PIECE, (at + 1) * PIECE)
        value_0 = mine_0[0, :, columns] + far_0[0, :, columns]
        value_1 = mine_1[0, :, columns] + far_1[0, :, columns]
        halves = jnp.where(first, value_0, value_1), jnp.where(first, value_1, value_0)
        for out, value in zip((near, away), halves):
            high, middle, low = split3(value)
            right = jnp.concatenate([high, middle, high, low, high, middle], axis=0)
            product = lax.dot_general(
                left, right, (((0,), (0,)), ((), ())), preferred_element_type=F32
            )
            for block in range(BLOCKS):
                out[at, m * BLOCKS + block] = product[:, block * 128 : (block + 1) * 128]


def right_product(core, packed, mine, far):
    wide_spec = pl.BlockSpec((1, ROWS, HALF), lambda m: (m, 0, 0))
    out_spec = pl.BlockSpec((NX, UNITS + 1, RANK, 128), lambda m: (0, 0, 0, 0))
    out_shape = jax.ShapeDtypeStruct((NX, UNITS + 1, RANK, 128), F32)
    return pl.pallas_call(
        right_kernel,
        grid=(3,),
        in_specs=[
            pl.BlockSpec(memory_space=pltpu.SMEM),
            pl.BlockSpec((1, 8, 128), lambda m: (m, 0, 0)),
        ]
        + [wide_spec] * 4,
        out_specs=[out_spec, out_spec],
        out_shape=[out_shape, out_shape],
        compiler_params=params(),
        name="right_product",
    )(core, packed, mine[0], far[0], mine[1], far[1])


def factor_kernel(gram, packed, inverse, p_factor):
    lane = lax.broadcasted_iota(jnp.int32, (3, RANK, RANK), 2)
    row = lax.broadcasted_iota(jnp.int32, (3, RANK, RANK), 1)
    wide = gram[...]
    left = jnp.stack(
        [wide[:, :RANK]] + [pltpu.roll(wide, 128 - RANK * m, 1)[:, :RANK] for m in (1, 2)]
    )
    right = jnp.where(lane == row, 1.0, 0.0).astype(F32)
    for step in range(RANK):
        pivot = left[:, step : step + 1, :]
        column = left[:, :, step : step + 1] / pivot[:, :, step : step + 1]
        scale = jnp.where(row[:, :, :1] > step, column, 0.0)
        right = right - scale * right[:, step : step + 1, :]
        left = left - scale * pivot
    diagonal = jnp.sum(jnp.where(lane == row, left, 0.0), axis=2, keepdims=True)
    result = right / jnp.sqrt(diagonal)
    inverse[...] = result
    for m in range(3):
        p_factor[m] = lax.dot_general(
            unpack_rows(packed[m])[:, :RANK],
            result[m],
            (((1,), (1,)), ((), ())),
            preferred_element_type=F32,
            precision=PRECISE,
        )


def factors(gram, packed):
    shape = jax.ShapeDtypeStruct((3, RANK, RANK), F32)
    return pl.pallas_call(
        factor_kernel,
        out_shape=[shape, shape],
        compiler_params=params(),
        name="factors",
    )(gram, packed)


def error_kernel(core_ref, q_near, q_far, p_factor, mine_0, far_0, mine_1, far_1, q_factor, error_next):
    first = core_ref[0] == 0
    left = jnp.concatenate(split3(p_factor[0]), axis=1)
    for at in range(NX):
        columns = slice(at * PIECE, (at + 1) * PIECE)
        near = jnp.concatenate([q_near[at, block] for block in range(BLOCKS)], axis=1)
        away = jnp.concatenate([q_far[at, block] for block in range(BLOCKS)], axis=1)
        halves = jnp.where(first, near, away), jnp.where(first, away, near)
        for half, mine, far in ((0, mine_0, far_0), (1, mine_1, far_1)):
            right = halves[half]
            there = slice(half * HALF + at * PIECE, half * HALF + (at + 1) * PIECE)
            q_factor[0, :, there] = right
            rebuilt = jnp.dot(
                left, jnp.concatenate([right] * 3, axis=0), preferred_element_type=F32
            )
            value = mine[0, :, columns] + far[0, :, columns]
            error_next[0, 0, :, there] = (value - rebuilt).astype(BF16)


def new_error(core, q_near, q_far, p_factor, mine, far):
    q_spec = pl.BlockSpec((NX, BLOCKS, RANK, 128), lambda m: (0, m, 0, 0))
    half_spec = pl.BlockSpec((1, ROWS, HALF), lambda m: (m, 0, 0))
    return pl.pallas_call(
        error_kernel,
        grid=(3,),
        in_specs=[
            pl.BlockSpec(memory_space=pltpu.SMEM),
            q_spec,
            q_spec,
            pl.BlockSpec((1, ROWS, RANK), lambda m: (m, 0, 0)),
        ]
        + [half_spec] * 4,
        out_specs=[
            pl.BlockSpec((1, RANK, D), lambda m: (m, 0, 0)),
            pl.BlockSpec((1, 1, ROWS, D), lambda m: (0, m, 0, 0)),
        ],
        out_shape=[
            jax.ShapeDtypeStruct((3, RANK, D), BF16),
            jax.ShapeDtypeStruct((1, 3, ROWS, D), BF16),
        ],
        compiler_params=params(),
        name="new_error",
    )(core, q_near, q_far, p_factor, mine[0], far[0], mine[1], far[1])


def spread(value, axis, count):
    copies = jnp.broadcast_to(value[None], (count,) + value.shape)
    return lax.all_to_all(copies, axis, 0, 0)


def swap_core(value):
    return lax.ppermute(value, "c", [(0, 1), (1, 0)])


def neighbour(at, way):
    return 3 - at if way else at ^ 1


def swap_chip(value, way):
    return lax.ppermute(value, "x", [(i, neighbour(i, way)) for i in range(NX)])


def exchange(inputs, out_grad, hidden, up_grad, gate_grad, error_memory, q_start):
    chip, core = lax.axis_index("x"), lax.axis_index("c")
    columns = jnp.concatenate([up_grad.T, gate_grad.T, hidden.T], axis=0)

    def tokens_of(first, second):
        starts = [(at * 2 + side) * 128 for at in (first, second) for side in (core, 1 - core)]
        return jnp.concatenate(
            [lax.dynamic_slice_in_dim(columns, start, 128, axis=1) for start in starts], axis=1
        )

    own, pair, u_self, u_far = [], [], [], []
    for way in range(2):
        here = slice(way * HALF, (way + 1) * HALF)
        own.append(jnp.stack([inputs[:, here], out_grad[:, here]]))
        pair.append(swap_chip(own[way], way))
    for way in range(2):
        partner = neighbour(chip, 1 - way)
        u_self.append(tokens_of(chip, neighbour(chip, way)))
        u_far.append(swap_chip(tokens_of(partner, neighbour(partner, way)), 1 - way))
    sibling = [swap_core(own[way]) for way in range(2)]
    mine, sent, packed, p_sent = [], [], [], []
    for way in range(2):
        results = partials(
            u_self[way],
            u_far[way],
            own[way],
            sibling[way],
            pair[way],
            swap_core(pair[way]),
            error_memory,
            q_start,
            way,
        )
        for values, value in zip((mine, sent, packed, p_sent), results):
            values.append(value)
    p_far = [swap_chip(p_sent[way], 1 - way) for way in range(2)]
    far = [swap_chip(sent[way], 1 - way) for way in range(2)]
    return mine, far, (packed[0] + packed[1]) + (p_far[0] + p_far[1])


def per_device(inputs, out_grad, hidden, up_grad, gate_grad, error_memory, q_start):
    core = lax.axis_index("c").reshape(1).astype(jnp.int32)
    mine, far, packed = exchange(
        inputs, out_grad, hidden, up_grad, gate_grad, error_memory, q_start
    )
    packed = spread(packed, "z", NZ).sum(0)
    packed = spread(packed, "y", NY).sum(0)

    near, away = right_product(core, packed, mine, far)
    w_core = near + swap_core(away)
    w_x = lax.all_to_all(w_core, "x", 0, 0).sum(0)
    inverse, p_factor = factors(w_x[UNITS], packed)
    w_y = lax.all_to_all(w_x.reshape(NY, 4, RANK, 128), "y", 0, 0).sum(0)
    unit_of = jnp.minimum((lax.axis_index("y") * 4 + jnp.arange(4)) // BLOCKS, 2)
    q_y = jnp.einsum("urs,usd->urd", inverse[unit_of], w_y, precision=PRECISE)
    q_z = lax.all_to_all(q_y.reshape(NZ, 8, 128), "z", 0, 0).sum(0)
    q_part = (q_z / (NY * NZ)).astype(BF16)

    q_dp = spread(q_part, "z", NZ).reshape(4, RANK, 128)
    q_near = spread(q_dp, ("x", "y"), NX * NY).reshape(NX, UNITS + 1, RANK, 128)
    q_factor, error_next = new_error(core, q_near, swap_core(q_near), p_factor, mine, far)
    return (error_next, p_factor, q_factor)


def solution(mesh):
    fine = Mesh(mesh.devices.reshape(NY, NZ, NX, NC), ("y", "z", "x", "c"))
    dp, tensor = ("y", "z"), ("x", "c")
    in_specs = (
        P(dp + tensor, None),
        P(dp + tensor, None),
        P(dp, tensor),
        P(dp, tensor),
        P(dp, tensor),
        P(dp, None, tensor, None),
        P(),
    )
    out_specs = (P(dp, None, tensor, None), P(None, tensor, None), P())
    return jax.shard_map(
        per_device, mesh=fine, in_specs=in_specs, out_specs=out_specs, check_vma=False
    )
```

```python
import jax
import jax.numpy as jnp
from jax import lax
from jax.experimental import pallas as pl
from jax.experimental.pallas import tpu as pltpu
from jax.sharding import Mesh, PartitionSpec as P

NY, NZ, NX, NC = 4, 16, 4, 2
SHARDS = NX * NC
D = 5120
RANK = 32
ROWS = 32
TOK = 1024
OWN = TOK // SHARDS
HALF = D // NC
PIECE = HALF // NX
BLOCKS = PIECE // 128
F32, BF16 = jnp.float32, jnp.bfloat16
VMEM_BYTES = 48 * 1024 * 1024
PRECISE = lax.Precision.HIGHEST
SMEM = pl.BlockSpec(memory_space=pltpu.SMEM)
ROWS_ON_ROWS = (((0,), (0,)), ((), ()))
LANES_ON_LANES = (((1,), (1,)), ((), ()))


def params():
    return pltpu.CompilerParams(vmem_limit_bytes=VMEM_BYTES)


def split3(value):
    high = value.astype(BF16)
    rest = value - high.astype(F32)
    middle = rest.astype(BF16)
    low = (rest - middle.astype(F32)).astype(BF16)
    return high, middle, low


def own_lanes(values):
    lane = lax.broadcasted_iota(jnp.int32, values[0].shape, 1)
    first = jnp.where(lane < RANK, values[0], values[1])
    return jnp.where(lane < 2 * RANK, first, jnp.where(lane < 3 * RANK, values[2], 0.0))


def token_kernel(inputs, out_grad, error, q_ref, token_q, error_q):
    @pl.when(pl.program_id(0) == 0)
    def _():
        token_q[...] = jnp.zeros_like(token_q)
        error_q[...] = jnp.zeros_like(error_q)

    width = inputs.shape[1]
    right = jnp.concatenate(
        [q_ref[0], q_ref[1], q_ref[2], jnp.zeros((128 - 3 * RANK, width), BF16)], axis=0
    )
    left = jnp.concatenate([inputs[...], out_grad[...], error[0, 0], error[0, 1], error[0, 2]], axis=0)
    product = lax.dot_general(left, right, LANES_ON_LANES, preferred_element_type=F32)
    of_inputs, of_out_grad, of_error = product[:OWN], product[OWN : 2 * OWN], product[2 * OWN :]
    token_q[...] += own_lanes([of_inputs, of_inputs, of_out_grad])
    error_q[...] += own_lanes([of_error[m * ROWS : (m + 1) * ROWS] for m in range(3)])


def token_products(inputs, out_grad, error, q_start):
    steps = 4
    width = D // steps
    x_spec = pl.BlockSpec((OWN, width), lambda i: (0, i))
    return pl.pallas_call(
        token_kernel,
        grid=(steps,),
        in_specs=[
            x_spec,
            x_spec,
            pl.BlockSpec((1, 3, ROWS, width), lambda i: (0, 0, 0, i)),
            pl.BlockSpec((3, RANK, width), lambda i: (0, 0, i)),
        ],
        out_specs=[
            pl.BlockSpec((OWN, 128), lambda i: (0, 0)),
            pl.BlockSpec((ROWS, 128), lambda i: (0, 0)),
        ],
        out_shape=[
            jax.ShapeDtypeStruct((OWN, 128), F32),
            jax.ShapeDtypeStruct((ROWS, 128), F32),
        ],
        compiler_params=params(),
        name="token_products",
    )(inputs, out_grad, error, q_start)


def left_kernel(shard_ref, units, token_q, error_q, p_part):
    rows = units[...].reshape(SHARDS * 3 * ROWS, OWN)
    product = jnp.zeros((SHARDS * 3 * ROWS, 128), F32)
    for part in split3(token_q[...])[::-1]:
        product = product + jnp.dot(rows, part, preferred_element_type=F32)
    for shard in range(SHARDS):
        at = shard * 3 * ROWS
        p_part[shard * ROWS : (shard + 1) * ROWS] = own_lanes(
            [product[at + m * ROWS : at + (m + 1) * ROWS] for m in range(3)]
        )
    mine = pl.ds(pl.multiple_of(shard_ref[0] * ROWS, ROWS), ROWS)
    p_part[mine] = p_part[mine] + error_q[...]


def left_product(shard, units, token_q, error_q):
    return pl.pallas_call(
        left_kernel,
        in_specs=[SMEM] + [pl.BlockSpec(memory_space=pltpu.VMEM)] * 3,
        out_shape=jax.ShapeDtypeStruct((SHARDS * ROWS, 128), F32),
        compiler_params=params(),
        name="left_product",
    )(shard, units, token_q, error_q)


def right_kernel(
    place, p_sum, units, x_near, x_away, o_near, o_away, e_near, e_away, near, away, token_p, error_p
):
    @pl.when(pl.program_id(0) == 0)
    def _():
        parts = split3(p_sum[...])
        for m in range(3):
            columns = jnp.concatenate(
                [units[shard, m * ROWS : (m + 1) * ROWS] for shard in range(SHARDS)], axis=0
            )
            total = jnp.zeros((128, OWN), F32)
            for part in parts[::-1]:
                total = total + lax.dot_general(
                    part, columns, ROWS_ON_ROWS, preferred_element_type=F32
                )
            token_p[m * RANK : (m + 1) * RANK] = jnp.concatenate(
                split3(total[m * RANK : (m + 1) * RANK]), axis=1
            )
        mine = p_sum[pl.ds(pl.multiple_of(place[1] * ROWS, ROWS), ROWS)]
        error_p[...] = jnp.concatenate(split3(mine), axis=0)

    for out, x_ref, o_ref, e_ref in ((near, x_near, o_near, e_near), (away, x_away, o_away, e_away)):
        branch = jnp.dot(
            token_p[: 2 * RANK], jnp.concatenate([x_ref[...]] * 3, axis=0), preferred_element_type=F32
        )
        down = jnp.dot(
            token_p[2 * RANK :], jnp.concatenate([o_ref[...]] * 3, axis=0), preferred_element_type=F32
        )
        for m, product in enumerate((branch[:RANK], branch[RANK:], down)):
            of_error = lax.dot_general(
                error_p[...],
                jnp.concatenate([e_ref[0, m]] * 3, axis=0),
                ROWS_ON_ROWS,
                preferred_element_type=F32,
            )
            product = product + of_error[m * RANK : (m + 1) * RANK]
            for block in range(BLOCKS):
                unit = m * BLOCKS + block
                out[0, unit // 4, unit % 4] = product[:, block * 128 : (block + 1) * 128]
        out[0, NY - 1, 3] = jnp.zeros((RANK, 128), F32)


def right_product(place, p_sum, units, inputs, out_grad, error):
    x_near = pl.BlockSpec((OWN, PIECE), lambda i, at: (0, at[0] * NX + i))
    x_away = pl.BlockSpec((OWN, PIECE), lambda i, at: (0, (1 - at[0]) * NX + i))
    e_near = pl.BlockSpec((1, 3, ROWS, PIECE), lambda i, at: (0, 0, 0, at[0] * NX + i))
    e_away = pl.BlockSpec((1, 3, ROWS, PIECE), lambda i, at: (0, 0, 0, (1 - at[0]) * NX + i))
    out_spec = pl.BlockSpec((1, NY, 4, RANK, 128), lambda i, at: (i, 0, 0, 0, 0))
    out_shape = jax.ShapeDtypeStruct((NX, NY, 4, RANK, 128), F32)
    return pl.pallas_call(
        right_kernel,
        grid_spec=pltpu.PrefetchScalarGridSpec(
            num_scalar_prefetch=1,
            grid=(NX,),
            in_specs=[
                pl.BlockSpec((SHARDS * ROWS, 128), lambda i, at: (0, 0)),
                pl.BlockSpec((SHARDS, 3 * ROWS, OWN), lambda i, at: (0, 0, 0)),
                x_near,
                x_away,
                x_near,
                x_away,
                e_near,
                e_away,
            ],
            out_specs=[out_spec, out_spec],
            scratch_shapes=[
                pltpu.VMEM((3 * RANK, 3 * OWN), BF16),
                pltpu.VMEM((3 * ROWS, 128), BF16),
            ],
        ),
        out_shape=[out_shape, out_shape],
        compiler_params=params(),
        name="right_product",
    )(place, p_sum, units, inputs, inputs, out_grad, out_grad, error, error)


def factor_kernel(place, p_sum, inverse, p_factor):
    lane = lax.broadcasted_iota(jnp.int32, (3, RANK, RANK), 2)
    row = lax.broadcasted_iota(jnp.int32, (3, RANK, RANK), 1)
    whole = p_sum[...]
    gram = lax.dot_general(
        whole, whole, ROWS_ON_ROWS, preferred_element_type=F32, precision=PRECISE
    )

    def columns_of(value, m):
        return (pltpu.roll(value, 128 - RANK * m, 1) if m else value)[:, :RANK]

    left = jnp.stack([columns_of(gram[m * RANK : (m + 1) * RANK], m) for m in range(3)])
    right = jnp.where(lane == row, 1.0, 0.0).astype(F32)
    for step in range(RANK):
        pivot = left[:, step : step + 1, :]
        column = left[:, :, step : step + 1] / pivot[:, :, step : step + 1]
        scale = jnp.where(row[:, :, :1] > step, column, 0.0)
        right = right - scale * right[:, step : step + 1, :]
        left = left - scale * pivot
    diagonal = jnp.sum(jnp.where(lane == row, left, 0.0), axis=2, keepdims=True)
    result = right / jnp.sqrt(diagonal)
    inverse[...] = result
    mine = p_sum[pl.ds(pl.multiple_of(place[1] * ROWS, ROWS), ROWS)]
    for m in range(3):
        p_factor[m] = lax.dot_general(
            columns_of(mine, m),
            result[m],
            LANES_ON_LANES,
            preferred_element_type=F32,
            precision=PRECISE,
        )


def factors(place, p_sum):
    shape = jax.ShapeDtypeStruct((3, RANK, RANK), F32)
    return pl.pallas_call(
        factor_kernel,
        in_specs=[SMEM, pl.BlockSpec(memory_space=pltpu.VMEM)],
        out_shape=[shape, shape],
        compiler_params=params(),
        name="factors",
    )(place, p_sum)


def scale_kernel(place, received, inverse, q_part):
    for slot in range(4):
        unit = place[2] * 4 + slot
        of_unit = jnp.where(
            unit < BLOCKS, inverse[0], jnp.where(unit < 2 * BLOCKS, inverse[1], inverse[2])
        )
        total = received[0, slot]
        for source in range(1, NX * NY):
            total = total + received[source, slot]
        q_part[slot] = jnp.dot(of_unit, total, preferred_element_type=F32, precision=PRECISE)


def scaled_sum(place, received, inverse):
    return pl.pallas_call(
        scale_kernel,
        in_specs=[SMEM] + [pl.BlockSpec(memory_space=pltpu.VMEM)] * 2,
        out_shape=jax.ShapeDtypeStruct((4, RANK, 128), F32),
        compiler_params=params(),
        name="scaled_sum",
    )(place, received, inverse)


def gradient_kernel(columns, tokens, error, matrices):
    product = jnp.dot(columns[...], tokens[...], preferred_element_type=F32)
    for k in range(matrices.shape[0]):
        matrices[k] = product[k * ROWS : (k + 1) * ROWS] + error[0, k].astype(F32)


def gradients(columns, tokens, error):
    count = columns.shape[0] // ROWS
    steps = 10
    width = D // steps
    first = 0 if count == 2 else 2
    return pl.pallas_call(
        gradient_kernel,
        grid=(steps,),
        in_specs=[
            pl.BlockSpec((count * ROWS, TOK), lambda i: (0, 0)),
            pl.BlockSpec((TOK, width), lambda i: (0, i)),
            pl.BlockSpec((1, count, ROWS, width), lambda i: (0, first // count, 0, i)),
        ],
        out_specs=pl.BlockSpec((count, ROWS, width), lambda i: (0, 0, i)),
        out_shape=jax.ShapeDtypeStruct((count, ROWS, D), F32),
        compiler_params=params(),
        name="gradients",
    )(columns, tokens, error)


def spread(value, axis, count):
    copies = jnp.broadcast_to(value[None], (count,) + value.shape)
    return lax.all_to_all(copies, axis, 0, 0)


def swap_core(value):
    return lax.ppermute(value, "c", [(0, 1), (1, 0)])


def error_kernel(place, q_near, q_far, p_factor, branch, down, q_factor, error_next):
    first = place[0] == 0
    for m in range(3):
        left = jnp.concatenate(split3(p_factor[m]), axis=1)
        for at in range(NX):
            units = range(m * BLOCKS, (m + 1) * BLOCKS)
            near = jnp.concatenate([q_near[at, unit] for unit in units], axis=1)
            away = jnp.concatenate([q_far[at, unit] for unit in units], axis=1)
            halves = jnp.where(first, near, away), jnp.where(first, away, near)
            for half, right in enumerate(halves):
                columns = slice(half * HALF + at * PIECE, half * HALF + (at + 1) * PIECE)
                q_factor[m, :, columns] = right
                rebuilt = jnp.dot(
                    left, jnp.concatenate([right] * 3, axis=0), preferred_element_type=F32
                )
                value = branch[m, :, columns] if m < 2 else down[0, :, columns]
                error_next[0, m, :, columns] = (value - rebuilt).astype(BF16)


def new_error(place, q_near, q_far, p_factor, branch, down):
    return pl.pallas_call(
        error_kernel,
        in_specs=[SMEM] + [pl.BlockSpec(memory_space=pltpu.VMEM)] * 5,
        out_shape=[
            jax.ShapeDtypeStruct((3, RANK, D), BF16),
            jax.ShapeDtypeStruct((1, 3, ROWS, D), BF16),
        ],
        compiler_params=params(),
        name="new_error",
    )(place, q_near, q_far, p_factor, branch, down)


def per_device(inputs, out_grad, hidden, up_grad, gate_grad, error_memory, q_start):
    core, row = lax.axis_index("c"), lax.axis_index("y")
    shard = lax.axis_index("x") * NC + core
    place = jnp.stack([core, shard, row]).astype(jnp.int32)
    tensor, scatter = ("x", "c"), ("x", "c", "y")
    all_inputs = lax.all_gather(inputs, tensor, axis=0, tiled=True)
    all_out_grad = lax.all_gather(out_grad, tensor, axis=0, tiled=True)

    columns = jnp.concatenate([up_grad.T, gate_grad.T, hidden.T], axis=0)
    units = columns.reshape(3 * ROWS, SHARDS, OWN).transpose(1, 0, 2)
    units = lax.all_to_all(units, tensor, 0, 0)
    token_q, error_q = token_products(inputs, out_grad, error_memory, q_start)
    p_part = left_product(place[1:2], units, token_q, error_q)
    p_rows = lax.all_to_all(p_part.reshape(SHARDS * NY, 8, 128), scatter, 0, 0).sum(0)
    p_rows = spread(p_rows, "z", NZ).sum(0)
    p_sum = spread(p_rows, scatter, SHARDS * NY).reshape(SHARDS * ROWS, 128)

    near, away = right_product(place, p_sum, units, inputs, out_grad, error_memory)
    w_core = (near + swap_core(away)).reshape(NX * NY, 4, RANK, 128)
    inverse, p_factor = factors(place, p_sum)
    received = lax.all_to_all(w_core, ("x", "y"), 0, 0)
    q_y = scaled_sum(place, received, inverse)
    q_z = lax.all_to_all(q_y.reshape(NZ, 8, 128), "z", 0, 0).sum(0)
    q_part = (q_z / (NY * NZ)).astype(BF16)

    q_dp = spread(q_part, "z", NZ).reshape(4, RANK, 128)
    q_near = spread(q_dp, ("x", "y"), NX * NY).reshape(NX, NY * 4, RANK, 128)

    branch = gradients(columns[: 2 * ROWS], all_inputs, error_memory)
    down = gradients(columns[2 * ROWS :], all_out_grad, error_memory)
    q_factor, error_next = new_error(place, q_near, swap_core(q_near), p_factor, branch, down)
    return (error_next, p_factor, q_factor)


def solution(mesh):
    fine = Mesh(mesh.devices.reshape(NY, NZ, NX, NC), ("y", "z", "x", "c"))
    dp, tensor = ("y", "z"), ("x", "c")
    in_specs = (
        P(dp + tensor, None),
        P(dp + tensor, None),
        P(dp, tensor),
        P(dp, tensor),
        P(dp, tensor),
        P(dp, None, tensor, None),
        P(),
    )
    out_specs = (P(dp, None, tensor, None), P(None, tensor, None), P())
    return jax.shard_map(
        per_device, mesh=fine, in_specs=in_specs, out_specs=out_specs, check_vma=False
    )
```

```python
import jax
import jax.numpy as jnp
from jax import lax
from jax.experimental import pallas as pl
from jax.experimental.pallas import tpu as pltpu
from jax.sharding import Mesh, PartitionSpec as P

NY, NZ, NX, NC = 4, 16, 4, 2
SHARDS = NX * NC
D = 5120
RANK = 32
ROWS = 32
TOK = 1024
OWN = TOK // SHARDS
HALF = D // NC
PIECE = HALF // NX
BLOCKS = PIECE // 128
TOKEN_STEPS = 2
F32, BF16 = jnp.float32, jnp.bfloat16
VMEM_BYTES = 48 * 1024 * 1024
WIDE_VMEM_BYTES = 60 * 1024 * 1024
PRECISE = lax.Precision.HIGHEST
SMEM = pl.BlockSpec(memory_space=pltpu.SMEM)
ROWS_ON_ROWS = (((0,), (0,)), ((), ()))
LANES_ON_LANES = (((1,), (1,)), ((), ()))


def params(limit=VMEM_BYTES):
    return pltpu.CompilerParams(vmem_limit_bytes=limit)


def split3(value):
    high = value.astype(BF16)
    rest = value - high.astype(F32)
    middle = rest.astype(BF16)
    low = (rest - middle.astype(F32)).astype(BF16)
    return high, middle, low


def own_lanes(values):
    lane = lax.broadcasted_iota(jnp.int32, values[0].shape, 1)
    first = jnp.where(lane < RANK, values[0], values[1])
    return jnp.where(lane < 2 * RANK, first, jnp.where(lane < 3 * RANK, values[2], 0.0))


def token_kernel(place, inputs, out_grad, error, q_ref, token_q, error_q, keep, sent):
    step = pl.program_id(0)

    @pl.when(step == 0)
    def _():
        token_q[...] = jnp.zeros_like(token_q)
        error_q[...] = jnp.zeros_like(error_q)

    for out, wanted in ((keep, step < TOKEN_STEPS // 2), (sent, step >= TOKEN_STEPS // 2)):

        @pl.when(wanted)
        def _(out=out):
            out[0] = inputs[...]
            out[1] = out_grad[...]

    width = inputs.shape[1]
    right = jnp.concatenate(
        [q_ref[0], q_ref[1], q_ref[2], jnp.zeros((128 - 3 * RANK, width), BF16)], axis=0
    )
    left = jnp.concatenate([inputs[...], out_grad[...], error[0, 0], error[0, 1], error[0, 2]], axis=0)
    product = lax.dot_general(left, right, LANES_ON_LANES, preferred_element_type=F32)
    of_inputs, of_out_grad, of_error = product[:OWN], product[OWN : 2 * OWN], product[2 * OWN :]
    token_q[...] += own_lanes([of_inputs, of_inputs, of_out_grad])
    error_q[...] += own_lanes([of_error[m * ROWS : (m + 1) * ROWS] for m in range(3)])


def token_products(place, inputs, out_grad, error, q_start):
    width = D // TOKEN_STEPS
    half = TOKEN_STEPS // 2

    def column(i, at):
        return (at[0] * half + i) % TOKEN_STEPS

    x_spec = pl.BlockSpec((OWN, width), lambda i, at: (0, column(i, at)))
    half_shape = jax.ShapeDtypeStruct((2, OWN, HALF), BF16)
    return pl.pallas_call(
        token_kernel,
        grid_spec=pltpu.PrefetchScalarGridSpec(
            num_scalar_prefetch=1,
            grid=(TOKEN_STEPS,),
            in_specs=[
                x_spec,
                x_spec,
                pl.BlockSpec((1, 3, ROWS, width), lambda i, at: (0, 0, 0, column(i, at))),
                pl.BlockSpec((3, RANK, width), lambda i, at: (0, 0, column(i, at))),
            ],
            out_specs=[
                pl.BlockSpec((OWN, 128), lambda i, at: (0, 0)),
                pl.BlockSpec((ROWS, 128), lambda i, at: (0, 0)),
                pl.BlockSpec((2, OWN, width), lambda i, at: (0, 0, jnp.minimum(i, half - 1))),
                pl.BlockSpec((2, OWN, width), lambda i, at: (0, 0, jnp.maximum(i - half, 0))),
            ],
        ),
        out_shape=[
            jax.ShapeDtypeStruct((OWN, 128), F32),
            jax.ShapeDtypeStruct((ROWS, 128), F32),
            half_shape,
            half_shape,
        ],
        compiler_params=params(),
        name="token_products",
    )(place, inputs, out_grad, error, q_start)


def left_kernel(shard_ref, units, token_q, error_q, p_part):
    rows = units[...].reshape(SHARDS * 3 * ROWS, OWN)
    product = jnp.zeros((SHARDS * 3 * ROWS, 128), F32)
    for part in split3(token_q[...])[::-1]:
        product = product + jnp.dot(rows, part, preferred_element_type=F32)
    for shard in range(SHARDS):
        at = shard * 3 * ROWS
        p_part[shard * ROWS : (shard + 1) * ROWS] = own_lanes(
            [product[at + m * ROWS : at + (m + 1) * ROWS] for m in range(3)]
        )
    mine = pl.ds(pl.multiple_of(shard_ref[0] * ROWS, ROWS), ROWS)
    p_part[mine] = p_part[mine] + error_q[...]


def left_product(shard, units, token_q, error_q):
    return pl.pallas_call(
        left_kernel,
        in_specs=[SMEM] + [pl.BlockSpec(memory_space=pltpu.VMEM)] * 3,
        out_shape=jax.ShapeDtypeStruct((SHARDS * ROWS, 128), F32),
        compiler_params=params(),
        name="left_product",
    )(shard, units, token_q, error_q)


def right_kernel(
    place, p_sum, units, x_near, x_away, o_near, o_away, e_near, e_away, near, away, token_p, error_p
):
    @pl.when(pl.program_id(0) == 0)
    def _():
        parts = split3(p_sum[...])
        for m in range(3):
            columns = jnp.concatenate(
                [units[shard, m * ROWS : (m + 1) * ROWS] for shard in range(SHARDS)], axis=0
            )
            total = jnp.zeros((128, OWN), F32)
            for part in parts[::-1]:
                total = total + lax.dot_general(
                    part, columns, ROWS_ON_ROWS, preferred_element_type=F32
                )
            token_p[m * RANK : (m + 1) * RANK] = jnp.concatenate(
                split3(total[m * RANK : (m + 1) * RANK]), axis=1
            )
        mine = p_sum[pl.ds(pl.multiple_of(place[1] * ROWS, ROWS), ROWS)]
        error_p[...] = jnp.concatenate(split3(mine), axis=0)

    for out, x_ref, o_ref, e_ref in ((near, x_near, o_near, e_near), (away, x_away, o_away, e_away)):
        branch = jnp.dot(
            token_p[: 2 * RANK], jnp.concatenate([x_ref[...]] * 3, axis=0), preferred_element_type=F32
        )
        down = jnp.dot(
            token_p[2 * RANK :], jnp.concatenate([o_ref[...]] * 3, axis=0), preferred_element_type=F32
        )
        for m, product in enumerate((branch[:RANK], branch[RANK:], down)):
            of_error = lax.dot_general(
                error_p[...],
                jnp.concatenate([e_ref[0, m]] * 3, axis=0),
                ROWS_ON_ROWS,
                preferred_element_type=F32,
            )
            product = product + of_error[m * RANK : (m + 1) * RANK]
            for block in range(BLOCKS):
                unit = m * BLOCKS + block
                out[0, unit // 4, unit % 4] = product[:, block * 128 : (block + 1) * 128]
        out[0, NY - 1, 3] = jnp.zeros((RANK, 128), F32)


def right_product(place, p_sum, units, inputs, out_grad, error):
    x_near = pl.BlockSpec((OWN, PIECE), lambda i, at: (0, at[0] * NX + i))
    x_away = pl.BlockSpec((OWN, PIECE), lambda i, at: (0, (1 - at[0]) * NX + i))
    e_near = pl.BlockSpec((1, 3, ROWS, PIECE), lambda i, at: (0, 0, 0, at[0] * NX + i))
    e_away = pl.BlockSpec((1, 3, ROWS, PIECE), lambda i, at: (0, 0, 0, (1 - at[0]) * NX + i))
    out_spec = pl.BlockSpec((1, NY, 4, RANK, 128), lambda i, at: (i, 0, 0, 0, 0))
    out_shape = jax.ShapeDtypeStruct((NX, NY, 4, RANK, 128), F32)
    return pl.pallas_call(
        right_kernel,
        grid_spec=pltpu.PrefetchScalarGridSpec(
            num_scalar_prefetch=1,
            grid=(NX,),
            in_specs=[
                pl.BlockSpec((SHARDS * ROWS, 128), lambda i, at: (0, 0)),
                pl.BlockSpec((SHARDS, 3 * ROWS, OWN), lambda i, at: (0, 0, 0)),
                x_near,
                x_away,
                x_near,
                x_away,
                e_near,
                e_away,
            ],
            out_specs=[out_spec, out_spec],
            scratch_shapes=[
                pltpu.VMEM((3 * RANK, 3 * OWN), BF16),
                pltpu.VMEM((3 * ROWS, 128), BF16),
            ],
        ),
        out_shape=[out_shape, out_shape],
        compiler_params=params(),
        name="right_product",
    )(place, p_sum, units, inputs, inputs, out_grad, out_grad, error, error)


def factor_kernel(place, p_sum, inverse, p_factor):
    lane = lax.broadcasted_iota(jnp.int32, (3, RANK, RANK), 2)
    row = lax.broadcasted_iota(jnp.int32, (3, RANK, RANK), 1)
    whole = p_sum[...]
    gram = lax.dot_general(
        whole, whole, ROWS_ON_ROWS, preferred_element_type=F32, precision=PRECISE
    )

    def columns_of(value, m):
        return (pltpu.roll(value, 128 - RANK * m, 1) if m else value)[:, :RANK]

    left = jnp.stack([columns_of(gram[m * RANK : (m + 1) * RANK], m) for m in range(3)])
    right = jnp.where(lane == row, 1.0, 0.0).astype(F32)
    for step in range(RANK):
        pivot = left[:, step : step + 1, :]
        column = left[:, :, step : step + 1] / pivot[:, :, step : step + 1]
        scale = jnp.where(row[:, :, :1] > step, column, 0.0)
        right = right - scale * right[:, step : step + 1, :]
        left = left - scale * pivot
    diagonal = jnp.sum(jnp.where(lane == row, left, 0.0), axis=2, keepdims=True)
    result = right / jnp.sqrt(diagonal)
    inverse[...] = result
    mine = p_sum[pl.ds(pl.multiple_of(place[1] * ROWS, ROWS), ROWS)]
    for m in range(3):
        p_factor[m] = lax.dot_general(
            columns_of(mine, m),
            result[m],
            LANES_ON_LANES,
            preferred_element_type=F32,
            precision=PRECISE,
        )


def factors(place, p_sum):
    shape = jax.ShapeDtypeStruct((3, RANK, RANK), F32)
    return pl.pallas_call(
        factor_kernel,
        in_specs=[SMEM, pl.BlockSpec(memory_space=pltpu.VMEM)],
        out_shape=[shape, shape],
        compiler_params=params(),
        name="factors",
    )(place, p_sum)


def scale_kernel(place, received, inverse, q_part):
    for slot in range(4):
        unit = place[2] * 4 + slot
        of_unit = jnp.where(
            unit < BLOCKS, inverse[0], jnp.where(unit < 2 * BLOCKS, inverse[1], inverse[2])
        )
        total = received[0, slot]
        for source in range(1, NX * NY):
            total = total + received[source, slot]
        q_part[slot] = jnp.dot(of_unit, total, preferred_element_type=F32, precision=PRECISE)


def scaled_sum(place, received, inverse):
    return pl.pallas_call(
        scale_kernel,
        in_specs=[SMEM] + [pl.BlockSpec(memory_space=pltpu.VMEM)] * 2,
        out_shape=jax.ShapeDtypeStruct((4, RANK, 128), F32),
        compiler_params=params(),
        name="scaled_sum",
    )(place, received, inverse)


def gradient_kernel(near, away, own, sibling, pair, pair_sibling, mine, beside, far):
    for at, first, last in ((0, 0, 2), (1, 2, 3)):
        tokens = jnp.concatenate([own[at], sibling[at], pair[at], pair_sibling[at]], axis=0)
        count = last - first
        columns = jnp.concatenate(
            [
                chip[side * 3 * ROWS + first * ROWS : side * 3 * ROWS + last * ROWS]
                for chip in (near, away)
                for side in range(NC)
            ],
            axis=0,
        )
        product = jnp.dot(columns, tokens, preferred_element_type=F32)
        for group, out in enumerate((mine, beside, far.at[0], far.at[1])):
            for k in range(count):
                start = (group * count + k) * ROWS
                out[first + k] = product[start : start + ROWS]


def gradients(near, away, tokens):
    steps = 2
    width = HALF // steps
    u_spec = pl.BlockSpec((NC * 3 * ROWS, 4 * OWN), lambda i: (0, 0))
    out_spec = pl.BlockSpec((3, ROWS, width), lambda i: (0, 0, i))
    shape = jax.ShapeDtypeStruct((3, ROWS, HALF), F32)
    return pl.pallas_call(
        gradient_kernel,
        grid=(steps,),
        in_specs=[u_spec, u_spec] + [pl.BlockSpec((2, OWN, width), lambda i: (0, 0, i))] * 4,
        out_specs=[
            out_spec,
            out_spec,
            pl.BlockSpec((NC, 3, ROWS, width), lambda i: (0, 0, 0, i)),
        ],
        out_shape=[shape, shape, jax.ShapeDtypeStruct((NC, 3, ROWS, HALF), F32)],
        compiler_params=params(WIDE_VMEM_BYTES),
        name="gradients",
    )(near, away, *tokens)


def spread(value, axis, count):
    copies = jnp.broadcast_to(value[None], (count,) + value.shape)
    return lax.all_to_all(copies, axis, 0, 0)


def swap_core(value):
    return lax.ppermute(value, "c", [(0, 1), (1, 0)])


def error_kernel(
    place, q_near, q_far, p_factor, mine, far, other, error, q_factor, error_next
):
    first = place[0] == 0
    for m in range(3):
        left = jnp.concatenate(split3(p_factor[m]), axis=1)
        for at in range(NX):
            units = range(m * BLOCKS, (m + 1) * BLOCKS)
            near = jnp.concatenate([q_near[at, unit] for unit in units], axis=1)
            away = jnp.concatenate([q_far[at, unit] for unit in units], axis=1)
            halves = jnp.where(first, near, away), jnp.where(first, away, near)
            piece = slice(at * PIECE, (at + 1) * PIECE)
            here = mine[m, :, piece] + far[0, m, :, piece]
            there = other[m, :, piece]
            values = jnp.where(first, here, there), jnp.where(first, there, here)
            for half in range(NC):
                right, value = halves[half], values[half]
                columns = slice(half * HALF + at * PIECE, half * HALF + (at + 1) * PIECE)
                q_factor[m, :, columns] = right
                rebuilt = jnp.dot(
                    left, jnp.concatenate([right] * 3, axis=0), preferred_element_type=F32
                )
                value = value + error[0, m, :, columns].astype(F32)
                error_next[0, m, :, columns] = (value - rebuilt).astype(BF16)


def new_error(place, q_near, q_far, p_factor, mine, far, other, error):
    return pl.pallas_call(
        error_kernel,
        in_specs=[SMEM] + [pl.BlockSpec(memory_space=pltpu.VMEM)] * 7,
        out_shape=[
            jax.ShapeDtypeStruct((3, RANK, D), BF16),
            jax.ShapeDtypeStruct((1, 3, ROWS, D), BF16),
        ],
        compiler_params=params(),
        name="new_error",
    )(place, q_near, q_far, p_factor, mine, far, other, error)


def partner(chip, core, step):
    return jnp.where(core == step, chip ^ 1, 3 - chip)


def swap_chip(value, step):
    perm = []
    for chip in range(NX):
        for core in range(NC):
            to = chip ^ 1 if core == step else 3 - chip
            perm.append((chip * NC + core, to * NC + core))
    return lax.ppermute(value, ("x", "c"), perm)


def pair_columns(columns, beside):
    chip, core = lax.axis_index("x"), lax.axis_index("c")
    both = jnp.concatenate([columns, beside], axis=0)

    def at_tokens_of(first):
        pair = (first, partner(first, core, 0))
        starts = [(at * NC + side) * OWN for at in pair for side in (core, 1 - core)]
        return jnp.concatenate(
            [lax.dynamic_slice_in_dim(both, start, OWN, axis=1) for start in starts], axis=1
        )

    return at_tokens_of(chip), swap_chip(at_tokens_of(partner(chip, core, 1)), 1)


def per_device(inputs, out_grad, hidden, up_grad, gate_grad, error_memory, q_start):
    core, row = lax.axis_index("c"), lax.axis_index("y")
    shard = lax.axis_index("x") * NC + core
    place = jnp.stack([core, shard, row]).astype(jnp.int32)
    tensor, scatter = ("x", "c"), ("x", "c", "y")
    token_q, error_q, keep, sent = token_products(
        place, inputs, out_grad, error_memory, q_start
    )
    sibling = swap_core(sent)

    columns = jnp.concatenate([up_grad.T, gate_grad.T, hidden.T], axis=0)
    units = columns.reshape(3 * ROWS, SHARDS, OWN).transpose(1, 0, 2)
    units = lax.all_to_all(units, tensor, 0, 0)
    p_part = left_product(place[1:2], units, token_q, error_q)
    p_rows = lax.all_to_all(p_part.reshape(SHARDS * NY, 8, 128), scatter, 0, 0).sum(0)
    p_rows, late_keep, late_sibling, late_columns = lax.optimization_barrier(
        (p_rows, keep, sibling, columns)
    )
    columns_beside = swap_core(late_columns)
    pair, pair_sibling = swap_chip(late_keep, 0), swap_chip(late_sibling, 0)
    p_rows = spread(p_rows, "z", NZ).sum(0)
    p_rows, columns_beside, pair = lax.optimization_barrier((p_rows, columns_beside, pair))
    u_near, u_away = pair_columns(columns, columns_beside)
    p_sum = spread(p_rows, scatter, SHARDS * NY).reshape(SHARDS * ROWS, 128)
    p_sum, u_away, pair_sibling = lax.optimization_barrier((p_sum, u_away, pair_sibling))

    near, away = right_product(place, p_sum, units, inputs, out_grad, error_memory)
    w_core = (near + swap_core(away)).reshape(NX * NY, 4, RANK, 128)
    inverse, p_factor = factors(place, p_sum)
    received = lax.all_to_all(w_core, ("x", "y"), 0, 0)
    mine, beside, away_sums = gradients(u_near, u_away, (keep, sibling, pair, pair_sibling))
    received, mine, beside, away_sums, inverse = lax.optimization_barrier(
        (received, mine, beside, away_sums, inverse)
    )
    far = swap_chip(away_sums, 1)
    q_y = scaled_sum(place, received, inverse)
    q_z = lax.all_to_all(q_y.reshape(NZ, 8, 128), "z", 0, 0).sum(0)
    q_part = (q_z / (NY * NZ)).astype(BF16)

    q_dp = spread(q_part, "z", NZ).reshape(4, RANK, 128)
    q_near = spread(q_dp, ("x", "y"), NX * NY).reshape(NX, NY * 4, RANK, 128)

    other = swap_core(beside + far[1])
    q_factor, error_next = new_error(
        place, q_near, swap_core(q_near), p_factor, mine, far, other, error_memory
    )
    return (error_next, p_factor, q_factor)


def solution(mesh):
    fine = Mesh(mesh.devices.reshape(NY, NZ, NX, NC), ("y", "z", "x", "c"))
    dp, tensor = ("y", "z"), ("x", "c")
    in_specs = (
        P(dp + tensor, None),
        P(dp + tensor, None),
        P(dp, tensor),
        P(dp, tensor),
        P(dp, tensor),
        P(dp, None, tensor, None),
        P(),
    )
    out_specs = (P(dp, None, tensor, None), P(None, tensor, None), P())
    return jax.shard_map(
        per_device, mesh=fine, in_specs=in_specs, out_specs=out_specs, check_vma=False
    )
```

```python
import jax
import jax.numpy as jnp
from jax import lax
from jax.experimental import pallas as pl
from jax.experimental.pallas import tpu as pltpu
from jax.sharding import Mesh, PartitionSpec as P

NY, NZ, NX, NC = 4, 16, 4, 2
SHARDS = NX * NC
D = 5120
RANK = 32
ROWS = 32
TOK = 1024
OWN = TOK // SHARDS
HALF = D // NC
PIECE = HALF // NX
BLOCKS = PIECE // 128
TOKEN_STEPS = 2
F32, BF16 = jnp.float32, jnp.bfloat16
VMEM_BYTES = 24 * 1024 * 1024
WIDE_VMEM_BYTES = 60 * 1024 * 1024
PRECISE = lax.Precision.HIGHEST
SMEM = pl.BlockSpec(memory_space=pltpu.SMEM)
ROWS_ON_ROWS = (((0,), (0,)), ((), ()))
LANES_ON_LANES = (((1,), (1,)), ((), ()))


def params(limit=VMEM_BYTES):
    return pltpu.CompilerParams(vmem_limit_bytes=limit)


def split3(value):
    high = value.astype(BF16)
    rest = value - high.astype(F32)
    middle = rest.astype(BF16)
    low = (rest - middle.astype(F32)).astype(BF16)
    return high, middle, low


def own_lanes(values):
    lane = lax.broadcasted_iota(jnp.int32, values[0].shape, 1)
    first = jnp.where(lane < RANK, values[0], values[1])
    return jnp.where(lane < 2 * RANK, first, jnp.where(lane < 3 * RANK, values[2], 0.0))


def token_kernel(place, inputs, out_grad, error, q_ref, token_q, error_q, keep, sent):
    step = pl.program_id(0)

    @pl.when(step == 0)
    def _():
        token_q[...] = jnp.zeros_like(token_q)
        error_q[...] = jnp.zeros_like(error_q)

    for out, wanted in ((keep, step < TOKEN_STEPS // 2), (sent, step >= TOKEN_STEPS // 2)):

        @pl.when(wanted)
        def _(out=out):
            out[0] = inputs[...]
            out[1] = out_grad[...]

    width = inputs.shape[1]
    right = jnp.concatenate(
        [q_ref[0], q_ref[1], q_ref[2], jnp.zeros((128 - 3 * RANK, width), BF16)], axis=0
    )
    left = jnp.concatenate([inputs[...], out_grad[...], error[0, 0], error[0, 1], error[0, 2]], axis=0)
    product = lax.dot_general(left, right, LANES_ON_LANES, preferred_element_type=F32)
    of_inputs, of_out_grad, of_error = product[:OWN], product[OWN : 2 * OWN], product[2 * OWN :]
    token_q[...] += own_lanes([of_inputs, of_inputs, of_out_grad])
    error_q[...] += own_lanes([of_error[m * ROWS : (m + 1) * ROWS] for m in range(3)])


def token_products(place, inputs, out_grad, error, q_start):
    width = D // TOKEN_STEPS
    half = TOKEN_STEPS // 2

    def column(i, at):
        return (at[0] * half + i) % TOKEN_STEPS

    x_spec = pl.BlockSpec((OWN, width), lambda i, at: (0, column(i, at)))
    half_shape = jax.ShapeDtypeStruct((2, OWN, HALF), BF16)
    return pl.pallas_call(
        token_kernel,
        grid_spec=pltpu.PrefetchScalarGridSpec(
            num_scalar_prefetch=1,
            grid=(TOKEN_STEPS,),
            in_specs=[
                x_spec,
                x_spec,
                pl.BlockSpec((1, 3, ROWS, width), lambda i, at: (0, 0, 0, column(i, at))),
                pl.BlockSpec((3, RANK, width), lambda i, at: (0, 0, column(i, at))),
            ],
            out_specs=[
                pl.BlockSpec((OWN, 128), lambda i, at: (0, 0)),
                pl.BlockSpec((ROWS, 128), lambda i, at: (0, 0)),
                pl.BlockSpec((2, OWN, width), lambda i, at: (0, 0, jnp.minimum(i, half - 1))),
                pl.BlockSpec((2, OWN, width), lambda i, at: (0, 0, jnp.maximum(i - half, 0))),
            ],
        ),
        out_shape=[
            jax.ShapeDtypeStruct((OWN, 128), F32),
            jax.ShapeDtypeStruct((ROWS, 128), F32),
            half_shape,
            half_shape,
        ],
        compiler_params=params(WIDE_VMEM_BYTES),
        name="token_products",
    )(place, inputs, out_grad, error, q_start)


def left_kernel(shard_ref, units, token_q, error_q, p_part):
    rows = units[...].reshape(SHARDS * 3 * ROWS, OWN)
    product = jnp.zeros((SHARDS * 3 * ROWS, 128), F32)
    for part in split3(token_q[...])[::-1]:
        product = product + jnp.dot(rows, part, preferred_element_type=F32)
    for shard in range(SHARDS):
        at = shard * 3 * ROWS
        p_part[shard * ROWS : (shard + 1) * ROWS] = own_lanes(
            [product[at + m * ROWS : at + (m + 1) * ROWS] for m in range(3)]
        )
    mine = pl.ds(pl.multiple_of(shard_ref[0] * ROWS, ROWS), ROWS)
    p_part[mine] = p_part[mine] + error_q[...]


def left_product(shard, units, token_q, error_q):
    return pl.pallas_call(
        left_kernel,
        in_specs=[SMEM] + [pl.BlockSpec(memory_space=pltpu.VMEM)] * 3,
        out_shape=jax.ShapeDtypeStruct((SHARDS * ROWS, 128), F32),
        compiler_params=params(),
        name="left_product",
    )(shard, units, token_q, error_q)


def right_half(token_p, error_p, x_ref, o_ref, e_ref, out):
    branch = jnp.dot(
        token_p[: 2 * RANK], jnp.concatenate([x_ref[...]] * 3, axis=0), preferred_element_type=F32
    )
    down = jnp.dot(
        token_p[2 * RANK :], jnp.concatenate([o_ref[...]] * 3, axis=0), preferred_element_type=F32
    )
    for m, product in enumerate((branch[:RANK], branch[RANK:], down)):
        rows = slice(m * RANK, (m + 1) * RANK)
        product = product + jnp.dot(
            error_p[rows], jnp.concatenate([e_ref[0, m]] * 3, axis=0), preferred_element_type=F32
        )
        for block in range(BLOCKS):
            unit = m * BLOCKS + block
            out[0, unit // 4, unit % 4] = product[:, block * 128 : (block + 1) * 128]
    out[0, NY - 1, 3] = jnp.zeros((RANK, 128), F32)


def away_kernel(place, p_sum, units, x_ref, o_ref, e_ref, out, token_p, error_p):
    @pl.when(pl.program_id(0) == 0)
    def _():
        columns = jnp.concatenate(
            [
                jnp.concatenate(
                    [units[shard, m * ROWS : (m + 1) * ROWS] for shard in range(SHARDS)], axis=0
                )
                for m in range(3)
            ],
            axis=1,
        )
        total = jnp.zeros((128, 3 * OWN), F32)
        for part in split3(p_sum[...].T)[::-1]:
            total = total + jnp.dot(part, columns, preferred_element_type=F32)
        for m in range(3):
            rows = slice(m * RANK, (m + 1) * RANK)
            token_p[rows] = jnp.concatenate(
                split3(total[rows, m * OWN : (m + 1) * OWN]), axis=1
            )
        mine = p_sum[pl.ds(pl.multiple_of(place[1] * ROWS, ROWS), ROWS)]
        error_p[...] = jnp.concatenate([part.T for part in split3(mine)], axis=1)

    right_half(token_p, error_p, x_ref, o_ref, e_ref, out)


def near_kernel(place, token_p, error_p, x_ref, o_ref, e_ref, out):
    right_half(token_p, error_p, x_ref, o_ref, e_ref, out)


def right_specs(stays):
    def column(i, at):
        return (at[0] if stays else 1 - at[0]) * NX + i

    x_spec = pl.BlockSpec((OWN, PIECE), lambda i, at: (0, column(i, at)))
    e_spec = pl.BlockSpec((1, 3, ROWS, PIECE), lambda i, at: (0, 0, 0, column(i, at)))
    out_spec = pl.BlockSpec((1, NY, 4, RANK, 128), lambda i, at: (i, 0, 0, 0, 0))
    token_spec = pl.BlockSpec((3 * RANK, 3 * OWN), lambda i, at: (0, 0))
    error_spec = pl.BlockSpec((128, 3 * ROWS), lambda i, at: (0, 0))
    return [x_spec, x_spec, e_spec], out_spec, [token_spec, error_spec]


RIGHT_SHAPE = jax.ShapeDtypeStruct((NX, NY, 4, RANK, 128), F32)


def right_away(place, p_sum, units, inputs, out_grad, error):
    blocks, out_spec, left_specs = right_specs(False)
    return pl.pallas_call(
        away_kernel,
        grid_spec=pltpu.PrefetchScalarGridSpec(
            num_scalar_prefetch=1,
            grid=(NX,),
            in_specs=[
                pl.BlockSpec((SHARDS * ROWS, 128), lambda i, at: (0, 0)),
                pl.BlockSpec((SHARDS, 3 * ROWS, OWN), lambda i, at: (0, 0, 0)),
            ]
            + blocks,
            out_specs=[out_spec] + left_specs,
        ),
        out_shape=[
            RIGHT_SHAPE,
            jax.ShapeDtypeStruct((3 * RANK, 3 * OWN), BF16),
            jax.ShapeDtypeStruct((128, 3 * ROWS), BF16),
        ],
        compiler_params=params(),
        name="right_away",
    )(place, p_sum, units, inputs, out_grad, error)


def right_near(place, token_p, error_p, inputs, out_grad, error):
    blocks, out_spec, left_specs = right_specs(True)
    return pl.pallas_call(
        near_kernel,
        grid_spec=pltpu.PrefetchScalarGridSpec(
            num_scalar_prefetch=1,
            grid=(NX,),
            in_specs=left_specs + blocks,
            out_specs=out_spec,
        ),
        out_shape=RIGHT_SHAPE,
        compiler_params=params(),
        name="right_near",
    )(place, token_p, error_p, inputs, out_grad, error)


def factor_kernel(place, p_sum, inverse, p_factor):
    lane = lax.broadcasted_iota(jnp.int32, (3, RANK, RANK), 2)
    row = lax.broadcasted_iota(jnp.int32, (3, RANK, RANK), 1)
    whole = p_sum[...]
    gram = lax.dot_general(
        whole, whole, ROWS_ON_ROWS, preferred_element_type=F32, precision=PRECISE
    )

    def columns_of(value, m):
        return (pltpu.roll(value, 128 - RANK * m, 1) if m else value)[:, :RANK]

    left = jnp.stack([columns_of(gram[m * RANK : (m + 1) * RANK], m) for m in range(3)])
    right = jnp.where(lane == row, 1.0, 0.0).astype(F32)
    for step in range(RANK):
        pivot = left[:, step : step + 1, :]
        column = left[:, :, step : step + 1] / pivot[:, :, step : step + 1]
        scale = jnp.where(row[:, :, :1] > step, column, 0.0)
        right = right - scale * right[:, step : step + 1, :]
        left = left - scale * pivot
    diagonal = jnp.sum(jnp.where(lane == row, left, 0.0), axis=2, keepdims=True)
    result = right / jnp.sqrt(diagonal)
    inverse[...] = result
    mine = p_sum[pl.ds(pl.multiple_of(place[1] * ROWS, ROWS), ROWS)]
    for m in range(3):
        p_factor[m] = lax.dot_general(
            columns_of(mine, m),
            result[m],
            LANES_ON_LANES,
            preferred_element_type=F32,
            precision=PRECISE,
        )


def factors(place, p_sum):
    shape = jax.ShapeDtypeStruct((3, RANK, RANK), F32)
    return pl.pallas_call(
        factor_kernel,
        in_specs=[SMEM, pl.BlockSpec(memory_space=pltpu.VMEM)],
        out_shape=[shape, shape],
        compiler_params=params(),
        name="factors",
    )(place, p_sum)


def scale_kernel(place, received, inverse, q_part):
    for slot in range(4):
        unit = place[2] * 4 + slot
        of_unit = jnp.where(
            unit < BLOCKS, inverse[0], jnp.where(unit < 2 * BLOCKS, inverse[1], inverse[2])
        )
        total = received[0, slot]
        for source in range(1, NX * NY):
            total = total + received[source, slot]
        q_part[slot] = jnp.dot(of_unit, total, preferred_element_type=F32, precision=PRECISE)


def scaled_sum(place, received, inverse):
    return pl.pallas_call(
        scale_kernel,
        in_specs=[SMEM] + [pl.BlockSpec(memory_space=pltpu.VMEM)] * 2,
        out_shape=jax.ShapeDtypeStruct((4, RANK, 128), F32),
        compiler_params=params(),
        name="scaled_sum",
    )(place, received, inverse)


def gradient_kernel(near, away, own, sibling, pair, pair_sibling, mine, beside, far):
    for at, first, last in ((0, 0, 2), (1, 2, 3)):
        tokens = jnp.concatenate([own[at], sibling[at], pair[at], pair_sibling[at]], axis=0)
        count = last - first
        columns = jnp.concatenate(
            [
                chip[side * 3 * ROWS + first * ROWS : side * 3 * ROWS + last * ROWS]
                for chip in (near, away)
                for side in range(NC)
            ],
            axis=0,
        )
        product = jnp.dot(columns, tokens, preferred_element_type=F32)
        for group, out in enumerate((mine, beside, far.at[0], far.at[1])):
            for k in range(count):
                start = (group * count + k) * ROWS
                out[first + k] = product[start : start + ROWS]


def gradients(near, away, tokens):
    steps = 2
    width = HALF // steps
    u_spec = pl.BlockSpec((NC * 3 * ROWS, 4 * OWN), lambda i: (0, 0))
    out_spec = pl.BlockSpec((3, ROWS, width), lambda i: (0, 0, i))
    shape = jax.ShapeDtypeStruct((3, ROWS, HALF), F32)
    return pl.pallas_call(
        gradient_kernel,
        grid=(steps,),
        in_specs=[u_spec, u_spec] + [pl.BlockSpec((2, OWN, width), lambda i: (0, 0, i))] * 4,
        out_specs=[
            out_spec,
            out_spec,
            pl.BlockSpec((NC, 3, ROWS, width), lambda i: (0, 0, 0, i)),
        ],
        out_shape=[shape, shape, jax.ShapeDtypeStruct((NC, 3, ROWS, HALF), F32)],
        compiler_params=params(WIDE_VMEM_BYTES),
        name="gradients",
    )(near, away, *tokens)


def spread(value, axis, count):
    copies = jnp.broadcast_to(value[None], (count,) + value.shape)
    return lax.all_to_all(copies, axis, 0, 0)


def swap_core(value):
    return lax.ppermute(value, "c", [(0, 1), (1, 0)])


def error_kernel(
    place, q_near, q_far, p_factor, mine, far, other, error, q_factor, error_next
):
    first = place[0] == 0
    for m in range(3):
        left = jnp.concatenate(split3(p_factor[m]), axis=1)
        for at in range(NX):
            units = range(m * BLOCKS, (m + 1) * BLOCKS)
            near = jnp.concatenate([q_near[at, unit] for unit in units], axis=1)
            away = jnp.concatenate([q_far[at, unit] for unit in units], axis=1)
            halves = jnp.where(first, near, away), jnp.where(first, away, near)
            piece = slice(at * PIECE, (at + 1) * PIECE)
            here = mine[m, :, piece] + far[0, m, :, piece]
            there = other[m, :, piece]
            values = jnp.where(first, here, there), jnp.where(first, there, here)
            for half in range(NC):
                right, value = halves[half], values[half]
                columns = slice(half * HALF + at * PIECE, half * HALF + (at + 1) * PIECE)
                q_factor[m, :, columns] = right
                rebuilt = jnp.dot(
                    left, jnp.concatenate([right] * 3, axis=0), preferred_element_type=F32
                )
                value = value + error[0, m, :, columns].astype(F32)
                error_next[0, m, :, columns] = (value - rebuilt).astype(BF16)


def new_error(place, q_near, q_far, p_factor, mine, far, other, error):
    return pl.pallas_call(
        error_kernel,
        in_specs=[SMEM] + [pl.BlockSpec(memory_space=pltpu.VMEM)] * 7,
        out_shape=[
            jax.ShapeDtypeStruct((3, RANK, D), BF16),
            jax.ShapeDtypeStruct((1, 3, ROWS, D), BF16),
        ],
        compiler_params=params(),
        name="new_error",
    )(place, q_near, q_far, p_factor, mine, far, other, error)


def partner(chip, core, step):
    return jnp.where(core == step, chip ^ 1, 3 - chip)


def swap_chip(value, step):
    perm = []
    for chip in range(NX):
        for core in range(NC):
            to = chip ^ 1 if core == step else 3 - chip
            perm.append((chip * NC + core, to * NC + core))
    return lax.ppermute(value, ("x", "c"), perm)


def pair_columns(columns, beside):
    chip, core = lax.axis_index("x"), lax.axis_index("c")
    both = jnp.concatenate([columns, beside], axis=0)

    def at_tokens_of(first):
        pair = (first, partner(first, core, 0))
        starts = [(at * NC + side) * OWN for at in pair for side in (core, 1 - core)]
        return jnp.concatenate(
            [lax.dynamic_slice_in_dim(both, start, OWN, axis=1) for start in starts], axis=1
        )

    return at_tokens_of(chip), swap_chip(at_tokens_of(partner(chip, core, 1)), 1)


def per_device(inputs, out_grad, hidden, up_grad, gate_grad, error_memory, q_start):
    core, row = lax.axis_index("c"), lax.axis_index("y")
    shard = lax.axis_index("x") * NC + core
    place = jnp.stack([core, shard, row]).astype(jnp.int32)
    tensor, scatter = ("x", "c"), ("x", "c", "y")
    token_q, error_q, keep, sent = token_products(
        place, inputs, out_grad, error_memory, q_start
    )

    columns = jnp.concatenate([up_grad.T, gate_grad.T, hidden.T], axis=0)
    units = columns.reshape(3 * ROWS, SHARDS, OWN).transpose(1, 0, 2)
    units = lax.all_to_all(units, tensor, 0, 0)
    p_part = left_product(place[1:2], units, token_q, error_q)
    p_part, late_sent = lax.optimization_barrier((p_part, sent))
    sibling = swap_core(late_sent)
    p_rows = lax.all_to_all(p_part.reshape(SHARDS * NY, 8, 128), scatter, 0, 0).sum(0)
    copies = jnp.broadcast_to(p_rows[None], (NZ,) + p_rows.shape)
    copies, late_keep, late_sibling, late_columns = lax.optimization_barrier(
        (copies, keep, sibling, columns)
    )
    pair, pair_sibling = swap_chip(late_keep, 0), swap_chip(late_sibling, 0)
    columns_beside = swap_core(late_columns)
    p_rows = lax.all_to_all(copies, "z", 0, 0).sum(0)
    p_rows, columns_beside, pair = lax.optimization_barrier((p_rows, columns_beside, pair))
    u_near, u_away = pair_columns(columns, columns_beside)
    p_sum = spread(p_rows, scatter, SHARDS * NY).reshape(SHARDS * ROWS, 128)
    p_sum, u_away, pair_sibling = lax.optimization_barrier((p_sum, u_away, pair_sibling))

    away, token_p, error_p = right_away(place, p_sum, units, inputs, out_grad, error_memory)
    near = right_near(place, token_p, error_p, inputs, out_grad, error_memory)
    w_core = (near + swap_core(away)).reshape(NX * NY, 4, RANK, 128)
    inverse, p_factor = factors(place, p_sum)
    received = lax.all_to_all(w_core, ("x", "y"), 0, 0)
    mine, beside, away_sums = gradients(u_near, u_away, (keep, sibling, pair, pair_sibling))
    received, mine, beside, away_sums, inverse = lax.optimization_barrier(
        (received, mine, beside, away_sums, inverse)
    )
    q_y = scaled_sum(place, received, inverse)
    q_y, away_sums = lax.optimization_barrier((q_y, away_sums))
    far = swap_chip(away_sums, 1)
    q_z = lax.all_to_all(q_y.reshape(NZ, 8, 128), "z", 0, 0).sum(0)
    q_part = (q_z / (NY * NZ)).astype(BF16)

    q_dp = spread(q_part, "z", NZ).reshape(4, RANK, 128)
    q_near = spread(q_dp, ("x", "y"), NX * NY).reshape(NX, NY * 4, RANK, 128)

    other = swap_core(beside + far[1])
    q_factor, error_next = new_error(
        place, q_near, swap_core(q_near), p_factor, mine, far, other, error_memory
    )
    return (error_next, p_factor, q_factor)


def solution(mesh):
    fine = Mesh(mesh.devices.reshape(NY, NZ, NX, NC), ("y", "z", "x", "c"))
    dp, tensor = ("y", "z"), ("x", "c")
    in_specs = (
        P(dp + tensor, None),
        P(dp + tensor, None),
        P(dp, tensor),
        P(dp, tensor),
        P(dp, tensor),
        P(dp, None, tensor, None),
        P(),
    )
    out_specs = (P(dp, None, tensor, None), P(None, tensor, None), P())
    return jax.shard_map(
        per_device, mesh=fine, in_specs=in_specs, out_specs=out_specs, check_vma=False
    )
```

```python
import jax
import jax.numpy as jnp
from jax import lax
from jax.experimental import pallas as pl
from jax.experimental.pallas import tpu as pltpu
from jax.sharding import Mesh, PartitionSpec as P

NY, NZ, NX, NC = 4, 16, 4, 2
SHARDS = NX * NC
D = 5120
RANK = 32
ROWS = 32
TOK = 1024
OWN = TOK // SHARDS
HALF = D // NC
PIECE = HALF // NX
BLOCKS = PIECE // 128
TOKEN_STEPS = 2
F32, BF16 = jnp.float32, jnp.bfloat16
VMEM_BYTES = 24 * 1024 * 1024
WIDE_VMEM_BYTES = 60 * 1024 * 1024
PRECISE = lax.Precision.HIGHEST
SMEM = pl.BlockSpec(memory_space=pltpu.SMEM)
ROWS_ON_ROWS = (((0,), (0,)), ((), ()))
LANES_ON_LANES = (((1,), (1,)), ((), ()))


def params(limit=VMEM_BYTES):
    return pltpu.CompilerParams(vmem_limit_bytes=limit)


def split3(value):
    high = value.astype(BF16)
    rest = value - high.astype(F32)
    middle = rest.astype(BF16)
    low = (rest - middle.astype(F32)).astype(BF16)
    return high, middle, low


def own_lanes(values):
    lane = lax.broadcasted_iota(jnp.int32, values[0].shape, 1)
    first = jnp.where(lane < RANK, values[0], values[1])
    return jnp.where(lane < 2 * RANK, first, jnp.where(lane < 3 * RANK, values[2], 0.0))


def token_kernel(place, inputs, out_grad, error, q_ref, token_q, error_q, keep, sent):
    step = pl.program_id(0)

    @pl.when(step == 0)
    def _():
        token_q[...] = jnp.zeros_like(token_q)
        error_q[...] = jnp.zeros_like(error_q)

    for out, wanted in ((keep, step < TOKEN_STEPS // 2), (sent, step >= TOKEN_STEPS // 2)):

        @pl.when(wanted)
        def _(out=out):
            out[0] = inputs[...]
            out[1] = out_grad[...]

    width = inputs.shape[1]
    right = jnp.concatenate(
        [q_ref[0], q_ref[1], q_ref[2], jnp.zeros((128 - 3 * RANK, width), BF16)], axis=0
    )
    left = jnp.concatenate([inputs[...], out_grad[...], error[0, 0], error[0, 1], error[0, 2]], axis=0)
    product = lax.dot_general(left, right, LANES_ON_LANES, preferred_element_type=F32)
    of_inputs, of_out_grad, of_error = product[:OWN], product[OWN : 2 * OWN], product[2 * OWN :]
    token_q[...] += own_lanes([of_inputs, of_inputs, of_out_grad])
    error_q[...] += own_lanes([of_error[m * ROWS : (m + 1) * ROWS] for m in range(3)])


def token_products(place, inputs, out_grad, error, q_start):
    width = D // TOKEN_STEPS
    half = TOKEN_STEPS // 2

    def column(i, at):
        return (at[0] * half + i) % TOKEN_STEPS

    x_spec = pl.BlockSpec((OWN, width), lambda i, at: (0, column(i, at)))
    half_shape = jax.ShapeDtypeStruct((2, OWN, HALF), BF16)
    return pl.pallas_call(
        token_kernel,
        grid_spec=pltpu.PrefetchScalarGridSpec(
            num_scalar_prefetch=1,
            grid=(TOKEN_STEPS,),
            in_specs=[
                x_spec,
                x_spec,
                pl.BlockSpec((1, 3, ROWS, width), lambda i, at: (0, 0, 0, column(i, at))),
                pl.BlockSpec((3, RANK, width), lambda i, at: (0, 0, column(i, at))),
            ],
            out_specs=[
                pl.BlockSpec((OWN, 128), lambda i, at: (0, 0)),
                pl.BlockSpec((ROWS, 128), lambda i, at: (0, 0)),
                pl.BlockSpec((2, OWN, width), lambda i, at: (0, 0, jnp.minimum(i, half - 1))),
                pl.BlockSpec((2, OWN, width), lambda i, at: (0, 0, jnp.maximum(i - half, 0))),
            ],
        ),
        out_shape=[
            jax.ShapeDtypeStruct((OWN, 128), F32),
            jax.ShapeDtypeStruct((ROWS, 128), F32),
            half_shape,
            half_shape,
        ],
        compiler_params=params(WIDE_VMEM_BYTES),
        name="token_products",
    )(place, inputs, out_grad, error, q_start)


def left_kernel(shard_ref, units, token_q, error_q, p_part):
    rows = units[...].reshape(SHARDS * 3 * ROWS, OWN)
    product = jnp.zeros((SHARDS * 3 * ROWS, 128), F32)
    for part in split3(token_q[...])[::-1]:
        product = product + jnp.dot(rows, part, preferred_element_type=F32)
    for shard in range(SHARDS):
        at = shard * 3 * ROWS
        p_part[shard * ROWS : (shard + 1) * ROWS] = own_lanes(
            [product[at + m * ROWS : at + (m + 1) * ROWS] for m in range(3)]
        )
    mine = pl.ds(pl.multiple_of(shard_ref[0] * ROWS, ROWS), ROWS)
    p_part[mine] = p_part[mine] + error_q[...]


def left_product(shard, units, token_q, error_q):
    return pl.pallas_call(
        left_kernel,
        in_specs=[SMEM] + [pl.BlockSpec(memory_space=pltpu.VMEM)] * 3,
        out_shape=jax.ShapeDtypeStruct((SHARDS * ROWS, 128), F32),
        compiler_params=params(),
        name="left_product",
    )(shard, units, token_q, error_q)


def right_half(token_p, error_p, x_ref, o_ref, e_ref, out):
    branch = jnp.dot(
        token_p[: 2 * RANK], jnp.concatenate([x_ref[...]] * 3, axis=0), preferred_element_type=F32
    )
    down = jnp.dot(
        token_p[2 * RANK :], jnp.concatenate([o_ref[...]] * 3, axis=0), preferred_element_type=F32
    )
    for m, product in enumerate((branch[:RANK], branch[RANK:], down)):
        rows = slice(m * RANK, (m + 1) * RANK)
        product = product + jnp.dot(
            error_p[rows], jnp.concatenate([e_ref[0, m]] * 3, axis=0), preferred_element_type=F32
        )
        for block in range(BLOCKS):
            unit = m * BLOCKS + block
            out[0, unit // 4, unit % 4] = product[:, block * 128 : (block + 1) * 128]
    out[0, NY - 1, 3] = jnp.zeros((RANK, 128), F32)


def away_kernel(core_ref, shard_ref, p_sum, units, x_ref, o_ref, e_ref, out, token_p, error_p):
    @pl.when(pl.program_id(0) == 0)
    def _():
        columns = jnp.concatenate(
            [
                jnp.concatenate(
                    [units[shard, m * ROWS : (m + 1) * ROWS] for shard in range(SHARDS)], axis=0
                )
                for m in range(3)
            ],
            axis=1,
        )
        total = jnp.zeros((128, 3 * OWN), F32)
        for part in split3(p_sum[...].T)[::-1]:
            total = total + jnp.dot(part, columns, preferred_element_type=F32)
        for m in range(3):
            rows = slice(m * RANK, (m + 1) * RANK)
            token_p[rows] = jnp.concatenate(
                split3(total[rows, m * OWN : (m + 1) * OWN]), axis=1
            )
        mine = p_sum[pl.ds(pl.multiple_of(shard_ref[0] * ROWS, ROWS), ROWS)]
        error_p[...] = jnp.concatenate([part.T for part in split3(mine)], axis=1)

    right_half(token_p, error_p, x_ref, o_ref, e_ref, out)


def near_kernel(place, token_p, error_p, x_ref, o_ref, e_ref, out):
    right_half(token_p, error_p, x_ref, o_ref, e_ref, out)


def right_specs(stays):
    def column(i, at):
        return (at[0] if stays else 1 - at[0]) * NX + i

    x_spec = pl.BlockSpec((OWN, PIECE), lambda i, at, *rest: (0, column(i, at)))
    e_spec = pl.BlockSpec((1, 3, ROWS, PIECE), lambda i, at, *rest: (0, 0, 0, column(i, at)))
    out_spec = pl.BlockSpec((1, NY, 4, RANK, 128), lambda i, *at: (i, 0, 0, 0, 0))
    token_spec = pl.BlockSpec((3 * RANK, 3 * OWN), lambda i, *at: (0, 0))
    error_spec = pl.BlockSpec((128, 3 * ROWS), lambda i, *at: (0, 0))
    return [x_spec, x_spec, e_spec], out_spec, [token_spec, error_spec]


RIGHT_SHAPE = jax.ShapeDtypeStruct((NX, NY, 4, RANK, 128), F32)


def right_away(core, shard, p_sum, units, inputs, out_grad, error):
    blocks, out_spec, left_specs = right_specs(False)
    return pl.pallas_call(
        away_kernel,
        grid_spec=pltpu.PrefetchScalarGridSpec(
            num_scalar_prefetch=2,
            grid=(NX,),
            in_specs=[
                pl.BlockSpec((SHARDS * ROWS, 128), lambda i, *at: (0, 0)),
                pl.BlockSpec((SHARDS, 3 * ROWS, OWN), lambda i, *at: (0, 0, 0)),
            ]
            + blocks,
            out_specs=[out_spec] + left_specs,
        ),
        out_shape=[
            RIGHT_SHAPE,
            jax.ShapeDtypeStruct((3 * RANK, 3 * OWN), BF16),
            jax.ShapeDtypeStruct((128, 3 * ROWS), BF16),
        ],
        compiler_params=params(),
        name="right_away",
    )(core, shard, p_sum, units, inputs, out_grad, error)


def right_near(core, token_p, error_p, inputs, out_grad, error):
    blocks, out_spec, left_specs = right_specs(True)
    return pl.pallas_call(
        near_kernel,
        grid_spec=pltpu.PrefetchScalarGridSpec(
            num_scalar_prefetch=1,
            grid=(NX,),
            in_specs=left_specs + blocks,
            out_specs=out_spec,
        ),
        out_shape=RIGHT_SHAPE,
        compiler_params=params(),
        name="right_near",
    )(core, token_p, error_p, inputs, out_grad, error)


def factor_kernel(shard_ref, p_sum, inverse, p_factor):
    lane = lax.broadcasted_iota(jnp.int32, (3, RANK, RANK), 2)
    row = lax.broadcasted_iota(jnp.int32, (3, RANK, RANK), 1)
    whole = p_sum[...]
    gram = lax.dot_general(
        whole, whole, ROWS_ON_ROWS, preferred_element_type=F32, precision=PRECISE
    )

    def columns_of(value, m):
        return (pltpu.roll(value, 128 - RANK * m, 1) if m else value)[:, :RANK]

    left = jnp.stack([columns_of(gram[m * RANK : (m + 1) * RANK], m) for m in range(3)])
    right = jnp.where(lane == row, 1.0, 0.0).astype(F32)
    for step in range(RANK):
        pivot = left[:, step : step + 1, :]
        column = left[:, :, step : step + 1] / pivot[:, :, step : step + 1]
        scale = jnp.where(row[:, :, :1] > step, column, 0.0)
        right = right - scale * right[:, step : step + 1, :]
        left = left - scale * pivot
    diagonal = jnp.sum(jnp.where(lane == row, left, 0.0), axis=2, keepdims=True)
    result = right / jnp.sqrt(diagonal)
    inverse[...] = result
    mine = p_sum[pl.ds(pl.multiple_of(shard_ref[0] * ROWS, ROWS), ROWS)]
    for m in range(3):
        p_factor[m] = lax.dot_general(
            columns_of(mine, m),
            result[m],
            LANES_ON_LANES,
            preferred_element_type=F32,
            precision=PRECISE,
        )


def factors(shard, p_sum):
    shape = jax.ShapeDtypeStruct((3, RANK, RANK), F32)
    return pl.pallas_call(
        factor_kernel,
        in_specs=[SMEM, pl.BlockSpec(memory_space=pltpu.VMEM)],
        out_shape=[shape, shape],
        compiler_params=params(),
        name="factors",
    )(shard, p_sum)


def scale_kernel(row_ref, received, inverse, q_part):
    for slot in range(4):
        unit = row_ref[0] * 4 + slot
        of_unit = jnp.where(
            unit < BLOCKS, inverse[0], jnp.where(unit < 2 * BLOCKS, inverse[1], inverse[2])
        )
        total = received[0, slot]
        for source in range(1, NX * NY):
            total = total + received[source, slot]
        q_part[slot] = jnp.dot(of_unit, total, preferred_element_type=F32, precision=PRECISE)


def scaled_sum(row, received, inverse):
    return pl.pallas_call(
        scale_kernel,
        in_specs=[SMEM] + [pl.BlockSpec(memory_space=pltpu.VMEM)] * 2,
        out_shape=jax.ShapeDtypeStruct((4, RANK, 128), F32),
        compiler_params=params(),
        name="scaled_sum",
    )(row, received, inverse)


def gradient_kernel(near, away, own, sibling, pair, pair_sibling, mine, beside, far):
    for at, first, last in ((0, 0, 2), (1, 2, 3)):
        tokens = jnp.concatenate([own[at], sibling[at], pair[at], pair_sibling[at]], axis=0)
        count = last - first
        columns = jnp.concatenate(
            [
                chip[side * 3 * ROWS + first * ROWS : side * 3 * ROWS + last * ROWS]
                for chip in (near, away)
                for side in range(NC)
            ],
            axis=0,
        )
        product = jnp.dot(columns, tokens, preferred_element_type=F32)
        for group, out in enumerate((mine, beside, far.at[0], far.at[1])):
            for k in range(count):
                start = (group * count + k) * ROWS
                out[first + k] = product[start : start + ROWS]


def gradients(near, away, tokens):
    steps = 2
    width = HALF // steps
    u_spec = pl.BlockSpec((NC * 3 * ROWS, 4 * OWN), lambda i: (0, 0))
    out_spec = pl.BlockSpec((3, ROWS, width), lambda i: (0, 0, i))
    shape = jax.ShapeDtypeStruct((3, ROWS, HALF), F32)
    return pl.pallas_call(
        gradient_kernel,
        grid=(steps,),
        in_specs=[u_spec, u_spec] + [pl.BlockSpec((2, OWN, width), lambda i: (0, 0, i))] * 4,
        out_specs=[
            out_spec,
            out_spec,
            pl.BlockSpec((NC, 3, ROWS, width), lambda i: (0, 0, 0, i)),
        ],
        out_shape=[shape, shape, jax.ShapeDtypeStruct((NC, 3, ROWS, HALF), F32)],
        compiler_params=params(WIDE_VMEM_BYTES),
        name="gradients",
    )(near, away, *tokens)


def spread(value, axis, count):
    copies = jnp.broadcast_to(value[None], (count,) + value.shape)
    return lax.all_to_all(copies, axis, 0, 0)


def swap_core(value):
    return lax.ppermute(value, "c", [(0, 1), (1, 0)])


def error_kernel(
    place, q_near, q_far, p_factor, mine, far, other, error, q_factor, error_next
):
    first = place[0] == 0
    for m in range(3):
        left = jnp.concatenate(split3(p_factor[m]), axis=1)
        for at in range(NX):
            units = range(m * BLOCKS, (m + 1) * BLOCKS)
            near = jnp.concatenate([q_near[at, unit] for unit in units], axis=1)
            away = jnp.concatenate([q_far[at, unit] for unit in units], axis=1)
            halves = jnp.where(first, near, away), jnp.where(first, away, near)
            piece = slice(at * PIECE, (at + 1) * PIECE)
            here = mine[m, :, piece] + far[0, m, :, piece]
            there = other[m, :, piece]
            values = jnp.where(first, here, there), jnp.where(first, there, here)
            for half in range(NC):
                right, value = halves[half], values[half]
                columns = slice(half * HALF + at * PIECE, half * HALF + (at + 1) * PIECE)
                q_factor[m, :, columns] = right
                rebuilt = jnp.dot(
                    left, jnp.concatenate([right] * 3, axis=0), preferred_element_type=F32
                )
                value = value + error[0, m, :, columns].astype(F32)
                error_next[0, m, :, columns] = (value - rebuilt).astype(BF16)


def new_error(place, q_near, q_far, p_factor, mine, far, other, error):
    return pl.pallas_call(
        error_kernel,
        in_specs=[SMEM] + [pl.BlockSpec(memory_space=pltpu.VMEM)] * 7,
        out_shape=[
            jax.ShapeDtypeStruct((3, RANK, D), BF16),
            jax.ShapeDtypeStruct((1, 3, ROWS, D), BF16),
        ],
        compiler_params=params(),
        name="new_error",
    )(place, q_near, q_far, p_factor, mine, far, other, error)


def partner(chip, core, step):
    return jnp.where(core == step, chip ^ 1, 3 - chip)


def swap_chip(value, step):
    perm = []
    for chip in range(NX):
        for core in range(NC):
            to = chip ^ 1 if core == step else 3 - chip
            perm.append((chip * NC + core, to * NC + core))
    return lax.ppermute(value, ("x", "c"), perm)


def swap_across(value):
    perm = []
    for chip in range(NX):
        for core in range(NC):
            to = chip ^ 1 if core == 1 else 3 - chip
            perm.append((chip * NC + core, to * NC + 1 - core))
    return lax.ppermute(value, ("x", "c"), perm)


def hidden_columns(up_grad, gate_grad, hidden):
    return jnp.concatenate([up_grad.T, gate_grad.T, hidden.T], axis=0)


def pair_columns(columns, beside):
    chip, core = lax.axis_index("x"), lax.axis_index("c")
    both = jnp.concatenate([columns, beside], axis=0)

    def at_tokens_of(first):
        pair = (first, partner(first, core, 0))
        starts = [(at * NC + side) * OWN for at in pair for side in (core, 1 - core)]
        return jnp.concatenate(
            [lax.dynamic_slice_in_dim(both, start, OWN, axis=1) for start in starts], axis=1
        )

    return at_tokens_of(chip), swap_chip(at_tokens_of(partner(chip, core, 1)), 1)


def per_device(inputs, out_grad, hidden, up_grad, gate_grad, error_memory, q_start):
    core, row = lax.axis_index("c"), lax.axis_index("y")
    shard = lax.axis_index("x") * NC + core
    core, shard, row = (at.reshape(1).astype(jnp.int32) for at in (core, shard, row))
    tensor, scatter = ("x", "c"), ("x", "c", "y")
    token_q, error_q, keep, sent = token_products(
        core, inputs, out_grad, error_memory, q_start
    )

    units = hidden_columns(up_grad, gate_grad, hidden)
    units = units.reshape(3 * ROWS, SHARDS, OWN).transpose(1, 0, 2)
    units = lax.all_to_all(units, tensor, 0, 0)
    p_part = left_product(shard, units, token_q, error_q)
    p_rows = lax.all_to_all(p_part.reshape(SHARDS * NY, 8, 128), scatter, 0, 0).sum(0)
    copies = jnp.broadcast_to(p_rows[None], (NZ,) + p_rows.shape)
    late = lax.optimization_barrier((copies, keep, sent, up_grad, gate_grad, hidden))
    copies, late_keep, late_sent = late[:3]
    late_columns = hidden_columns(*late[3:])
    pair, pair_sibling = swap_chip(late_keep, 0), swap_across(late_sent)
    columns_beside = swap_core(late_columns)
    p_rows = lax.all_to_all(copies, "z", 0, 0).sum(0)
    p_rows, columns_beside = lax.optimization_barrier((p_rows, columns_beside))
    u_near, u_away = pair_columns(late_columns, columns_beside)
    p_sum = spread(p_rows, scatter, SHARDS * NY).reshape(SHARDS * ROWS, 128)
    p_sum, u_away, pair, pair_sibling, late_sent = lax.optimization_barrier(
        (p_sum, u_away, pair, pair_sibling, late_sent)
    )
    sibling = swap_core(late_sent)

    away, token_p, error_p = right_away(core, shard, p_sum, units, inputs, out_grad, error_memory)
    near = right_near(core, token_p, error_p, inputs, out_grad, error_memory)
    w_core = (near + swap_core(away)).reshape(NX * NY, 4, RANK, 128)
    inverse, p_factor = factors(shard, p_sum)
    received = lax.all_to_all(w_core, ("x", "y"), 0, 0)
    mine, beside, away_sums = gradients(u_near, u_away, (keep, sibling, pair, pair_sibling))
    received, mine, beside, away_sums, inverse = lax.optimization_barrier(
        (received, mine, beside, away_sums, inverse)
    )
    q_y = scaled_sum(row, received, inverse)
    q_y, away_sums = lax.optimization_barrier((q_y, away_sums))
    far = swap_chip(away_sums, 1)
    q_z = lax.all_to_all(q_y.reshape(NZ, 8, 128), "z", 0, 0).sum(0)
    q_part = (q_z / (NY * NZ)).astype(BF16)

    q_dp = spread(q_part, "z", NZ).reshape(4, RANK, 128)
    q_near = spread(q_dp, ("x", "y"), NX * NY).reshape(NX, NY * 4, RANK, 128)

    other = swap_core(beside + far[1])
    q_factor, error_next = new_error(
        core, q_near, swap_core(q_near), p_factor, mine, far, other, error_memory
    )
    return (error_next, p_factor, q_factor)


def solution(mesh):
    fine = Mesh(mesh.devices.reshape(NY, NZ, NX, NC), ("y", "z", "x", "c"))
    dp, tensor = ("y", "z"), ("x", "c")
    in_specs = (
        P(dp + tensor, None),
        P(dp + tensor, None),
        P(dp, tensor),
        P(dp, tensor),
        P(dp, tensor),
        P(dp, None, tensor, None),
        P(),
    )
    out_specs = (P(dp, None, tensor, None), P(None, tensor, None), P())
    return jax.shard_map(
        per_device, mesh=fine, in_specs=in_specs, out_specs=out_specs, check_vma=False
    )
```

```python
import jax
import jax.numpy as jnp
from jax import lax
from jax.experimental import pallas as pl
from jax.experimental.pallas import tpu as pltpu
from jax.sharding import Mesh, PartitionSpec as P

NY, NZ, NX, NC = 4, 16, 4, 2
SHARDS = NX * NC
D = 5120
RANK = 32
ROWS = 32
TOK = 1024
OWN = TOK // SHARDS
HALF = D // NC
PIECE = HALF // NX
BLOCKS = PIECE // 128
TOKEN_STEPS = 4
F32, BF16 = jnp.float32, jnp.bfloat16
VMEM_BYTES = 24 * 1024 * 1024
WIDE_VMEM_BYTES = 60 * 1024 * 1024
PRECISE = lax.Precision.HIGHEST
SMEM = pl.BlockSpec(memory_space=pltpu.SMEM)
ROWS_ON_ROWS = (((0,), (0,)), ((), ()))
LANES_ON_LANES = (((1,), (1,)), ((), ()))


def params(limit=VMEM_BYTES):
    return pltpu.CompilerParams(vmem_limit_bytes=limit)


def split3(value):
    high = value.astype(BF16)
    rest = value - high.astype(F32)
    middle = rest.astype(BF16)
    low = (rest - middle.astype(F32)).astype(BF16)
    return high, middle, low


def own_lanes(values):
    lane = lax.broadcasted_iota(jnp.int32, values[0].shape, 1)
    first = jnp.where(lane < RANK, values[0], values[1])
    return jnp.where(lane < 2 * RANK, first, jnp.where(lane < 3 * RANK, values[2], 0.0))


def token_kernel(place, inputs, out_grad, error, q_ref, token_q, error_q, keep, sent):
    step = pl.program_id(0)

    @pl.when(step == 0)
    def _():
        token_q[...] = jnp.zeros_like(token_q)
        error_q[...] = jnp.zeros_like(error_q)

    for out, wanted in ((keep, step < TOKEN_STEPS // 2), (sent, step >= TOKEN_STEPS // 2)):

        @pl.when(wanted)
        def _(out=out):
            out[0] = inputs[...]
            out[1] = out_grad[...]

    width = inputs.shape[1]
    right = jnp.concatenate(
        [q_ref[0], q_ref[1], q_ref[2], jnp.zeros((128 - 3 * RANK, width), BF16)], axis=0
    )
    left = jnp.concatenate([inputs[...], out_grad[...], error[0, 0], error[0, 1], error[0, 2]], axis=0)
    product = lax.dot_general(left, right, LANES_ON_LANES, preferred_element_type=F32)
    of_inputs, of_out_grad, of_error = product[:OWN], product[OWN : 2 * OWN], product[2 * OWN :]
    token_q[...] += own_lanes([of_inputs, of_inputs, of_out_grad])
    error_q[...] += own_lanes([of_error[m * ROWS : (m + 1) * ROWS] for m in range(3)])


def token_products(place, inputs, out_grad, error, q_start):
    width = D // TOKEN_STEPS
    half = TOKEN_STEPS // 2

    def column(i, at):
        return (at[0] * half + i) % TOKEN_STEPS

    x_spec = pl.BlockSpec((OWN, width), lambda i, at: (0, column(i, at)))
    half_shape = jax.ShapeDtypeStruct((2, OWN, HALF), BF16)
    return pl.pallas_call(
        token_kernel,
        grid_spec=pltpu.PrefetchScalarGridSpec(
            num_scalar_prefetch=1,
            grid=(TOKEN_STEPS,),
            in_specs=[
                x_spec,
                x_spec,
                pl.BlockSpec((1, 3, ROWS, width), lambda i, at: (0, 0, 0, column(i, at))),
                pl.BlockSpec((3, RANK, width), lambda i, at: (0, 0, column(i, at))),
            ],
            out_specs=[
                pl.BlockSpec((OWN, 128), lambda i, at: (0, 0)),
                pl.BlockSpec((ROWS, 128), lambda i, at: (0, 0)),
                pl.BlockSpec((2, OWN, width), lambda i, at: (0, 0, jnp.minimum(i, half - 1))),
                pl.BlockSpec((2, OWN, width), lambda i, at: (0, 0, jnp.maximum(i - half, 0))),
            ],
        ),
        out_shape=[
            jax.ShapeDtypeStruct((OWN, 128), F32),
            jax.ShapeDtypeStruct((ROWS, 128), F32),
            half_shape,
            half_shape,
        ],
        compiler_params=params(WIDE_VMEM_BYTES),
        name="token_products",
    )(place, inputs, out_grad, error, q_start)


def left_kernel(shard_ref, units, token_q, error_q, p_part):
    rows = units[...].reshape(SHARDS * 3 * ROWS, OWN)
    product = jnp.zeros((SHARDS * 3 * ROWS, 128), F32)
    for part in split3(token_q[...])[::-1]:
        product = product + jnp.dot(rows, part, preferred_element_type=F32)
    for shard in range(SHARDS):
        at = shard * 3 * ROWS
        p_part[shard * ROWS : (shard + 1) * ROWS] = own_lanes(
            [product[at + m * ROWS : at + (m + 1) * ROWS] for m in range(3)]
        )
    mine = pl.ds(pl.multiple_of(shard_ref[0] * ROWS, ROWS), ROWS)
    p_part[mine] = p_part[mine] + error_q[...]


def left_product(shard, units, token_q, error_q):
    return pl.pallas_call(
        left_kernel,
        in_specs=[SMEM] + [pl.BlockSpec(memory_space=pltpu.VMEM)] * 3,
        out_shape=jax.ShapeDtypeStruct((SHARDS * ROWS, 128), F32),
        compiler_params=params(),
        name="left_product",
    )(shard, units, token_q, error_q)


def right_half(token_p, error_p, x_ref, o_ref, e_ref, out):
    branch = jnp.dot(
        token_p[: 2 * RANK], jnp.concatenate([x_ref[...]] * 3, axis=0), preferred_element_type=F32
    )
    down = jnp.dot(
        token_p[2 * RANK :], jnp.concatenate([o_ref[...]] * 3, axis=0), preferred_element_type=F32
    )
    for m, product in enumerate((branch[:RANK], branch[RANK:], down)):
        rows = slice(m * RANK, (m + 1) * RANK)
        product = product + jnp.dot(
            error_p[rows], jnp.concatenate([e_ref[0, m]] * 3, axis=0), preferred_element_type=F32
        )
        for block in range(BLOCKS):
            unit = m * BLOCKS + block
            out[0, unit // 4, unit % 4] = product[:, block * 128 : (block + 1) * 128]
    out[0, NY - 1, 3] = jnp.zeros((RANK, 128), F32)


def away_kernel(core_ref, shard_ref, p_sum, units, x_ref, o_ref, e_ref, out, token_p, error_p):
    @pl.when(pl.program_id(0) == 0)
    def _():
        columns = jnp.concatenate(
            [
                jnp.concatenate(
                    [units[shard, m * ROWS : (m + 1) * ROWS] for shard in range(SHARDS)], axis=0
                )
                for m in range(3)
            ],
            axis=1,
        )
        total = jnp.zeros((128, 3 * OWN), F32)
        for part in split3(p_sum[...].T)[::-1]:
            total = total + jnp.dot(part, columns, preferred_element_type=F32)
        for m in range(3):
            rows = slice(m * RANK, (m + 1) * RANK)
            token_p[rows] = jnp.concatenate(
                split3(total[rows, m * OWN : (m + 1) * OWN]), axis=1
            )
        mine = p_sum[pl.ds(pl.multiple_of(shard_ref[0] * ROWS, ROWS), ROWS)]
        error_p[...] = jnp.concatenate([part.T for part in split3(mine)], axis=1)

    right_half(token_p, error_p, x_ref, o_ref, e_ref, out)


def near_kernel(place, token_p, error_p, x_ref, o_ref, e_ref, out):
    right_half(token_p, error_p, x_ref, o_ref, e_ref, out)


def right_specs(stays):
    def column(i, at):
        return (at[0] if stays else 1 - at[0]) * NX + i

    x_spec = pl.BlockSpec((OWN, PIECE), lambda i, at, *rest: (0, column(i, at)))
    e_spec = pl.BlockSpec((1, 3, ROWS, PIECE), lambda i, at, *rest: (0, 0, 0, column(i, at)))
    out_spec = pl.BlockSpec((1, NY, 4, RANK, 128), lambda i, *at: (i, 0, 0, 0, 0))
    token_spec = pl.BlockSpec((3 * RANK, 3 * OWN), lambda i, *at: (0, 0))
    error_spec = pl.BlockSpec((128, 3 * ROWS), lambda i, *at: (0, 0))
    return [x_spec, x_spec, e_spec], out_spec, [token_spec, error_spec]


RIGHT_SHAPE = jax.ShapeDtypeStruct((NX, NY, 4, RANK, 128), F32)


def right_away(core, shard, p_sum, units, inputs, out_grad, error):
    blocks, out_spec, left_specs = right_specs(False)
    return pl.pallas_call(
        away_kernel,
        grid_spec=pltpu.PrefetchScalarGridSpec(
            num_scalar_prefetch=2,
            grid=(NX,),
            in_specs=[
                pl.BlockSpec((SHARDS * ROWS, 128), lambda i, *at: (0, 0)),
                pl.BlockSpec((SHARDS, 3 * ROWS, OWN), lambda i, *at: (0, 0, 0)),
            ]
            + blocks,
            out_specs=[out_spec] + left_specs,
        ),
        out_shape=[
            RIGHT_SHAPE,
            jax.ShapeDtypeStruct((3 * RANK, 3 * OWN), BF16),
            jax.ShapeDtypeStruct((128, 3 * ROWS), BF16),
        ],
        compiler_params=params(),
        name="right_away",
    )(core, shard, p_sum, units, inputs, out_grad, error)


def right_near(core, token_p, error_p, inputs, out_grad, error):
    blocks, out_spec, left_specs = right_specs(True)
    return pl.pallas_call(
        near_kernel,
        grid_spec=pltpu.PrefetchScalarGridSpec(
            num_scalar_prefetch=1,
            grid=(NX,),
            in_specs=left_specs + blocks,
            out_specs=out_spec,
        ),
        out_shape=RIGHT_SHAPE,
        compiler_params=params(),
        name="right_near",
    )(core, token_p, error_p, inputs, out_grad, error)


def factor_kernel(shard_ref, p_sum, inverse, p_factor):
    lane = lax.broadcasted_iota(jnp.int32, (3, RANK, RANK), 2)
    row = lax.broadcasted_iota(jnp.int32, (3, RANK, RANK), 1)
    whole = p_sum[...]
    gram = lax.dot_general(
        whole, whole, ROWS_ON_ROWS, preferred_element_type=F32, precision=PRECISE
    )

    def columns_of(value, m):
        return (pltpu.roll(value, 128 - RANK * m, 1) if m else value)[:, :RANK]

    left = jnp.stack([columns_of(gram[m * RANK : (m + 1) * RANK], m) for m in range(3)])
    right = jnp.where(lane == row, 1.0, 0.0).astype(F32)
    for step in range(RANK):
        pivot = left[:, step : step + 1, :]
        column = left[:, :, step : step + 1] / pivot[:, :, step : step + 1]
        scale = jnp.where(row[:, :, :1] > step, column, 0.0)
        right = right - scale * right[:, step : step + 1, :]
        left = left - scale * pivot
    diagonal = jnp.sum(jnp.where(lane == row, left, 0.0), axis=2, keepdims=True)
    result = right / jnp.sqrt(diagonal)
    inverse[...] = result
    mine = p_sum[pl.ds(pl.multiple_of(shard_ref[0] * ROWS, ROWS), ROWS)]
    for m in range(3):
        p_factor[m] = lax.dot_general(
            columns_of(mine, m),
            result[m],
            LANES_ON_LANES,
            preferred_element_type=F32,
            precision=PRECISE,
        )


def factors(shard, p_sum):
    shape = jax.ShapeDtypeStruct((3, RANK, RANK), F32)
    return pl.pallas_call(
        factor_kernel,
        in_specs=[SMEM, pl.BlockSpec(memory_space=pltpu.VMEM)],
        out_shape=[shape, shape],
        compiler_params=params(),
        name="factors",
    )(shard, p_sum)


def scale_kernel(row_ref, received, inverse, q_part):
    for slot in range(4):
        unit = row_ref[0] * 4 + slot
        of_unit = jnp.where(
            unit < BLOCKS, inverse[0], jnp.where(unit < 2 * BLOCKS, inverse[1], inverse[2])
        )
        total = received[0, slot]
        for source in range(1, NX * NY):
            total = total + received[source, slot]
        q_part[slot] = jnp.dot(of_unit, total, preferred_element_type=F32, precision=PRECISE)


def scaled_sum(row, received, inverse):
    return pl.pallas_call(
        scale_kernel,
        in_specs=[SMEM] + [pl.BlockSpec(memory_space=pltpu.VMEM)] * 2,
        out_shape=jax.ShapeDtypeStruct((4, RANK, 128), F32),
        compiler_params=params(),
        name="scaled_sum",
    )(row, received, inverse)


def gradient_kernel(near, away, own, sibling, pair, pair_sibling, mine, beside, far):
    for at, first, last in ((0, 0, 2), (1, 2, 3)):
        tokens = jnp.concatenate([own[at], sibling[at], pair[at], pair_sibling[at]], axis=0)
        count = last - first
        columns = jnp.concatenate(
            [
                chip[side * 3 * ROWS + first * ROWS : side * 3 * ROWS + last * ROWS]
                for chip in (near, away)
                for side in range(NC)
            ],
            axis=0,
        )
        product = jnp.dot(columns, tokens, preferred_element_type=F32)
        for group, out in enumerate((mine, beside, far.at[0], far.at[1])):
            for k in range(count):
                start = (group * count + k) * ROWS
                out[first + k] = product[start : start + ROWS]


def gradients(near, away, tokens):
    steps = 2
    width = HALF // steps
    u_spec = pl.BlockSpec((NC * 3 * ROWS, 4 * OWN), lambda i: (0, 0))
    out_spec = pl.BlockSpec((3, ROWS, width), lambda i: (0, 0, i))
    shape = jax.ShapeDtypeStruct((3, ROWS, HALF), F32)
    return pl.pallas_call(
        gradient_kernel,
        grid=(steps,),
        in_specs=[u_spec, u_spec] + [pl.BlockSpec((2, OWN, width), lambda i: (0, 0, i))] * 4,
        out_specs=[
            out_spec,
            out_spec,
            pl.BlockSpec((NC, 3, ROWS, width), lambda i: (0, 0, 0, i)),
        ],
        out_shape=[shape, shape, jax.ShapeDtypeStruct((NC, 3, ROWS, HALF), F32)],
        compiler_params=params(WIDE_VMEM_BYTES),
        name="gradients",
    )(near, away, *tokens)


def spread(value, axis, count):
    copies = jnp.broadcast_to(value[None], (count,) + value.shape)
    return lax.all_to_all(copies, axis, 0, 0)


def swap_core(value):
    return lax.ppermute(value, "c", [(0, 1), (1, 0)])


def error_kernel(
    place, q_near, q_far, p_factor, mine, far, other, error, q_factor, error_next
):
    first = place[0] == 0
    for m in range(3):
        left = jnp.concatenate(split3(p_factor[m]), axis=1)
        for at in range(NX):
            units = range(m * BLOCKS, (m + 1) * BLOCKS)
            near = jnp.concatenate([q_near[at, unit] for unit in units], axis=1)
            away = jnp.concatenate([q_far[at, unit] for unit in units], axis=1)
            halves = jnp.where(first, near, away), jnp.where(first, away, near)
            piece = slice(at * PIECE, (at + 1) * PIECE)
            here = mine[m, :, piece] + far[0, m, :, piece]
            there = other[m, :, piece]
            values = jnp.where(first, here, there), jnp.where(first, there, here)
            for half in range(NC):
                right, value = halves[half], values[half]
                columns = slice(half * HALF + at * PIECE, half * HALF + (at + 1) * PIECE)
                q_factor[m, :, columns] = right
                rebuilt = jnp.dot(
                    left, jnp.concatenate([right] * 3, axis=0), preferred_element_type=F32
                )
                value = value + error[0, m, :, columns].astype(F32)
                error_next[0, m, :, columns] = (value - rebuilt).astype(BF16)


def new_error(place, q_near, q_far, p_factor, mine, far, other, error):
    return pl.pallas_call(
        error_kernel,
        in_specs=[SMEM] + [pl.BlockSpec(memory_space=pltpu.VMEM)] * 7,
        out_shape=[
            jax.ShapeDtypeStruct((3, RANK, D), BF16),
            jax.ShapeDtypeStruct((1, 3, ROWS, D), BF16),
        ],
        compiler_params=params(),
        name="new_error",
    )(place, q_near, q_far, p_factor, mine, far, other, error)


def partner(chip, core, step):
    return jnp.where(core == step, chip ^ 1, 3 - chip)


def swap_chip(value, step):
    perm = []
    for chip in range(NX):
        for core in range(NC):
            to = chip ^ 1 if core == step else 3 - chip
            perm.append((chip * NC + core, to * NC + core))
    return lax.ppermute(value, ("x", "c"), perm)


def swap_across(value):
    perm = []
    for chip in range(NX):
        for core in range(NC):
            to = chip ^ 1 if core == 1 else 3 - chip
            perm.append((chip * NC + core, to * NC + 1 - core))
    return lax.ppermute(value, ("x", "c"), perm)


def hidden_columns(up_grad, gate_grad, hidden):
    return jnp.concatenate([up_grad.T, gate_grad.T, hidden.T], axis=0)


def pair_columns(columns, beside):
    chip, core = lax.axis_index("x"), lax.axis_index("c")
    both = jnp.concatenate([columns, beside], axis=0)

    def at_tokens_of(first):
        pair = (first, partner(first, core, 0))
        starts = [(at * NC + side) * OWN for at in pair for side in (core, 1 - core)]
        return jnp.concatenate(
            [lax.dynamic_slice_in_dim(both, start, OWN, axis=1) for start in starts], axis=1
        )

    return at_tokens_of(chip), swap_chip(at_tokens_of(partner(chip, core, 1)), 1)


def per_device(inputs, out_grad, hidden, up_grad, gate_grad, error_memory, q_start):
    core, row = lax.axis_index("c"), lax.axis_index("y")
    shard = lax.axis_index("x") * NC + core
    core, shard, row = (at.reshape(1).astype(jnp.int32) for at in (core, shard, row))
    tensor, scatter = ("x", "c"), ("x", "c", "y")
    token_q, error_q, keep, sent = token_products(
        core, inputs, out_grad, error_memory, q_start
    )

    units = hidden_columns(up_grad, gate_grad, hidden)
    units = units.reshape(3 * ROWS, SHARDS, OWN).transpose(1, 0, 2)
    units = lax.all_to_all(units, tensor, 0, 0)
    p_part = left_product(shard, units, token_q, error_q)
    p_rows = lax.all_to_all(p_part.reshape(SHARDS * NY, 8, 128), scatter, 0, 0).sum(0)
    copies = jnp.broadcast_to(p_rows[None], (NZ,) + p_rows.shape)
    late = lax.optimization_barrier((copies, keep, sent, up_grad, gate_grad, hidden))
    copies, late_keep, late_sent = late[:3]
    late_columns = hidden_columns(*late[3:])
    pair, pair_sibling = swap_chip(late_keep, 0), swap_across(late_sent)
    columns_beside = swap_core(late_columns)
    p_rows = lax.all_to_all(copies, "z", 0, 0).sum(0)
    p_rows, columns_beside = lax.optimization_barrier((p_rows, columns_beside))
    u_near, u_away = pair_columns(late_columns, columns_beside)
    p_sum = spread(p_rows, scatter, SHARDS * NY).reshape(SHARDS * ROWS, 128)
    p_sum, u_away, pair, pair_sibling, late_sent = lax.optimization_barrier(
        (p_sum, u_away, pair, pair_sibling, late_sent)
    )
    sibling = swap_core(late_sent)

    away, token_p, error_p = right_away(core, shard, p_sum, units, inputs, out_grad, error_memory)
    near = right_near(core, token_p, error_p, inputs, out_grad, error_memory)
    w_core = (near + swap_core(away)).reshape(NX * NY, 4, RANK, 128)
    inverse, p_factor = factors(shard, p_sum)
    received = lax.all_to_all(w_core, ("x", "y"), 0, 0)
    mine, beside, away_sums = gradients(u_near, u_away, (keep, sibling, pair, pair_sibling))
    received, mine, beside, away_sums, inverse = lax.optimization_barrier(
        (received, mine, beside, away_sums, inverse)
    )
    q_y = scaled_sum(row, received, inverse)
    q_y, away_sums = lax.optimization_barrier((q_y, away_sums))
    far = swap_chip(away_sums, 1)
    q_z = lax.all_to_all(q_y.reshape(NZ, 8, 128), "z", 0, 0).sum(0)
    q_part = (q_z / (NY * NZ)).astype(BF16)

    q_dp = spread(q_part, "z", NZ).reshape(4, RANK, 128)
    q_near = spread(q_dp, ("x", "y"), NX * NY).reshape(NX, NY * 4, RANK, 128)

    other = swap_core(beside + far[1])
    q_factor, error_next = new_error(
        core, q_near, swap_core(q_near), p_factor, mine, far, other, error_memory
    )
    return (error_next, p_factor, q_factor)


def solution(mesh):
    fine = Mesh(mesh.devices.reshape(NY, NZ, NX, NC), ("y", "z", "x", "c"))
    dp, tensor = ("y", "z"), ("x", "c")
    in_specs = (
        P(dp + tensor, None),
        P(dp + tensor, None),
        P(dp, tensor),
        P(dp, tensor),
        P(dp, tensor),
        P(dp, None, tensor, None),
        P(),
    )
    out_specs = (P(dp, None, tensor, None), P(None, tensor, None), P())
    return jax.shard_map(
        per_device, mesh=fine, in_specs=in_specs, out_specs=out_specs, check_vma=False
    )
```
